256 devices in a mesh: seq: 64 (over y_hi, z, x), blk: 4 (over y_lo, core).
Axes of the slice: x: 4, y: 4 (y_hi: 2, y_lo: 2; y = y_hi * 2 + y_lo), z: 8, core: 2. Of those that a mesh axis runs over, the one named last changes fastest.
Arguments:
- lin_query: bfloat16 [8192, 4096], P('seq', 'blk'), may hold values from -6 to 6
- lin_key: bfloat16 [8192, 4096], P('seq', 'blk'), may hold values from -6 to 6
- lin_value: bfloat16 [8192, 4096], P('seq', 'blk'), may hold values from -6 to 6
- log_decay: float32 [32, 8192], P('blk', 'seq'), may hold values from -1.5 to 0, as said below
- norm_gain: float32 [4096], P('blk'), may hold values from 0.1 to 1.9
- soft_query: bfloat16 [8192, 4096], P('seq', 'blk'), may hold values from -60 to 60
- span_kv: bfloat16 [8192, 2, 4, 128], P('seq', None, 'blk'), may hold values from -6 to 6
- cache_kv: bfloat16 [4096, 2, 4, 128], P('blk'), may hold values from -6 to 6
- cache_lens: int32 [4], replicated, may hold values from 1 to 1024, 3072 in all
- span_start: int32 [1], replicated, may hold values from 3072 to 7167
Outputs:
- linear_out: bfloat16 [8192, 4096], P('seq', 'blk')
- attended: bfloat16 [8192, 4096], P('seq', 'blk')
The draws below stay inside these ranges and needn't reach their ends.
Inputs may be any that keep to these rules, and one draw needn't show every extreme that they name: `log_decay`: every entry is below zero. Slots 0 to cache_lens[b] - 1 of shard b hold the cached prefix; the shard's later slots are empty.
All inputs are finite; a program needn't handle non-finite values.
Results may differ from the reference program's by a relative error of at most 0.029.
Values may be sent and summed in bfloat16 or wider, within the bound.
A program may use at most 128 MiB of HBM per device.

```python
import math
import jax
import jax.numpy as jnp
import numpy as np
from jax import lax

HEADS = 32
KV_HEADS = 4
HEAD = 128
TOK_DEV = 128
CAP = 1024
SPAN = 8192
N_BLK = 4


def draw_soft_query(key, part):
    key = jax.random.fold_in(key, 7)
    values_out = jnp.clip(jax.random.normal(key, (SPAN, HEADS, HEAD), jnp.float32), -6.0, 6.0)
    return values_out.reshape(SPAN, HEADS * HEAD).astype(jnp.bfloat16)


def draw_cache_kv(key, part):
    key = jax.random.fold_in(key, 13)
    shape_all = (N_BLK * CAP, 2, KV_HEADS, HEAD)
    values_out = jnp.clip(jax.random.normal(key, shape_all, jnp.float32), -6.0, 6.0)
    return values_out.astype(jnp.bfloat16)


def draw_log_decay(key, part):
    key = jax.random.fold_in(key, 29)
    streams = jax.random.split(key, 7)
    slow_share = 0.5
    slow_heads = jax.random.bernoulli(streams[0], slow_share, (HEADS, 1))
    slow_rate = jax.random.uniform(streams[1], (HEADS, 1), jnp.float32, 0.1, 0.2) * (2.3 / SPAN)
    fast_rate = jnp.exp(-jax.random.uniform(streams[2], (HEADS, 1), jnp.float32, math.log(30.0), math.log(50.0)))
    fading_speed_constant = jnp.where(slow_heads, slow_rate, fast_rate)
    group_count = SPAN // TOK_DEV
    cluster_scaling_factor = jnp.exp(jax.random.uniform(streams[3], (HEADS, group_count, 1), jnp.float32, math.log(0.6), math.log(1.5)))
    cluster_scaling_factor = jnp.broadcast_to(cluster_scaling_factor, (HEADS, group_count, TOK_DEV)).reshape(HEADS, SPAN)
    unit_scaling_factor = jnp.exp(jax.random.uniform(streams[4], (HEADS, SPAN), jnp.float32, math.log(0.5), math.log(2.0)))
    location_places = jax.random.randint(streams[5], (HEADS, 2), 0, SPAN)
    retain_indicator = jax.random.uniform(streams[6], (HEADS, 2), jnp.float32, 0.5, 0.8)
    element_location = jnp.arange(SPAN, dtype=jnp.int32)
    sequence_runs = jnp.sum(jnp.where(element_location[None, :, None] == location_places[:, None, :], jnp.log(retain_indicator)[:, None, :], 0.0), axis=2)
    return -fading_speed_constant * cluster_scaling_factor * unit_scaling_factor + sequence_runs


def level_of(key, dims, pieces, low, high):
    def one(position, parts):
        steps = jax.random.uniform(jax.random.fold_in(jax.random.fold_in(key, 6), position), (parts,), jnp.float32, low / len(pieces), high / len(pieces))
        return jnp.repeat(jnp.exp(steps), dims[position] // parts).reshape((-1,) + (1,) * (len(dims) - position - 1))

    loudness = one(*pieces[0])
    for cut in pieces[1:]:
        loudness = loudness * one(*cut)
    return loudness


def split_up(count, total, bound, skew):
    loads = [(1 << 20) // math.isqrt(standing ** skew) + 1 for standing in range(2, count + 1)]
    spare, counts = total - bound - (count - 1), [1] * (count - 1)
    while spare > 0:
        movable = [i for i in range(count - 1) if counts[i] < bound]
        pool, budget = sum([loads[i] for i in movable]), spare
        for i in movable:
            more = min(bound - counts[i], max(1, budget * loads[i] // pool), spare)
            counts[i] = counts[i] + more
            spare = spare - more
    return np.array([bound] + counts)


def ragged_sizes(rng, count, total, limit, lean):
    if count == 2:
        one = jax.random.randint(rng, (), max(1, total - limit), min(limit, total - 1) + 1)
        return jnp.stack([one, total - one])
    lengths = jnp.asarray(split_up(count, total, limit, lean), jnp.int32)
    couples = (count - 1) // 2
    giver, sink = lengths[1:1 + 2 * couples:2], lengths[2:2 + 2 * couples:2]
    slack = jnp.minimum(giver - 1, limit - sink)
    moved = jax.random.randint(jax.random.fold_in(rng, 1), (couples,), 0, 1 << 20) % (slack + 1)
    lengths = lengths.at[1:1 + 2 * couples:2].set(giver - moved).at[2:2 + 2 * couples:2].set(sink + moved)
    return lengths[jax.random.permutation(jax.random.fold_in(rng, 2), count)]


def centred(stream_key, dims, deviation, most, cuts=(), held_as=jnp.bfloat16):
    array = jax.random.normal(stream_key, dims, jnp.float32) * deviation
    if len(cuts) > 0:
        array = level_of(stream_key, dims, cuts, -0.22, 0.18) * array
    return jnp.clip(array, min=-most, max=most).astype(held_as)


def setup_inputs(seed: int = 0) -> dict:
    streams_of = jax.random.split(jax.random.key(seed), 11)
    lin_query = centred(streams_of[0], (SPAN, HEADS * HEAD), 1.0, 6.0, ((0, 64), (1, 4)))
    lin_key = centred(streams_of[1], (SPAN, HEADS * HEAD), 1.0, 6.0, ((0, 64), (1, 4)))
    lin_value = centred(streams_of[2], (SPAN, HEADS * HEAD), 1.0, 6.0, ((0, 64), (1, 4)))
    log_decay = draw_log_decay(jax.random.fold_in(streams_of[10], 71), 0)
    norm_gain = jnp.clip(1.0 + 0.18 * jax.random.normal(streams_of[4], (HEADS * HEAD,), jnp.float32), 0.1, 1.9)
    soft_query = draw_soft_query(jax.random.fold_in(streams_of[10], 71), 0)
    span_kv = centred(streams_of[6], (SPAN, 2, KV_HEADS, HEAD), 1.0, 6.0, ((0, 64), (2, 4)))
    cache_kv = draw_cache_kv(jax.random.fold_in(streams_of[10], 71), 0)
    cache_lens = ragged_sizes(streams_of[8], N_BLK, (N_BLK - 1) * CAP, CAP, 0).astype(jnp.int32)
    span_start = jax.random.randint(streams_of[9], (1,), (N_BLK - 1) * CAP, (N_BLK - 1) * CAP + 4096).astype(jnp.int32)
    return {"lin_query": lin_query, "lin_key": lin_key, "lin_value": lin_value, "log_decay": log_decay, "norm_gain": norm_gain, "soft_query": soft_query, "span_kv": span_kv, "cache_kv": cache_kv, "cache_lens": cache_lens, "span_start": span_start}


rotary_rates = (10000000.0 ** (-np.arange(32) / 32.0)).astype(np.float32)
epsilon = 1e-06
highest = lax.Precision.HIGHEST
score_scale = 1.0 / math.sqrt(128.0)

def rotate(features, positions):
    angles = positions[:, None] * jnp.asarray(rotary_rates)[None, :]
    cosine = jnp.cos(angles)[:, None, :]
    sine_term = jnp.sin(angles)[:, None, :]
    leading = features[:, :, :32]
    trailing = features[:, :, 32:64]
    return jnp.concatenate([leading * cosine - trailing * sine_term, trailing * cosine + leading * sine_term, features[:, :, 64:]], axis=2)

def normalize(outputs, norm_gain):
    root_mean = jnp.sqrt(lax.optimization_barrier(jnp.mean(outputs * outputs, axis=2, keepdims=True)) + epsilon)
    scaled = outputs / root_mean * norm_gain.reshape(1, outputs.shape[1], outputs.shape[2])
    return scaled.reshape(outputs.shape[0], outputs.shape[1] * outputs.shape[2]).astype(jnp.bfloat16)

def block_terms(queries, key_rows, value_rows, decays, carried_state):
    cumulative = jnp.cumsum(decays, axis=1)
    length = queries.shape[0]
    positions = jnp.arange(length, dtype=jnp.int32)
    causal = positions[:, None] >= positions[None, :]
    scores = jnp.einsum('thd,uhd->htu', queries.astype(jnp.float32), key_rows.astype(jnp.float32))
    differences = cumulative[:, :, None] - cumulative[:, None, :]
    weights = jnp.where(causal[None], jnp.exp(jnp.minimum(differences, 0.0)), 0.0)
    values_wide = value_rows.astype(jnp.float32)
    within = jnp.einsum('htu,uhd->thd', scores * weights, values_wide, precision=highest)
    scaled = queries.astype(jnp.float32) * jnp.exp(cumulative).T[:, :, None]
    carried = jnp.einsum('thd,hde->the', scaled, carried_state, precision=highest)
    tail_decay = jnp.exp(cumulative[:, -1:] - cumulative).T[:, :, None]
    local_state = jnp.einsum('thd,the->hde', key_rows.astype(jnp.float32) * tail_decay, values_wide, precision=highest)
    new_state = jnp.exp(cumulative[:, -1])[:, None, None] * carried_state + local_state
    return (within + carried, new_state)

def lightning(lin_query, lin_key, lin_value, log_decay, norm_gain):
    head_count = log_decay.shape[0]
    row_total = lin_query.shape[0]
    group_count = row_total // TOK_DEV

    def blocked(source):
        return source.reshape(group_count, TOK_DEV, head_count, HEAD)
    decays = log_decay.reshape(head_count, group_count, TOK_DEV).transpose(1, 0, 2)

    def advance(carried_state, inputs):
        outputs, carried_state = block_terms(inputs[0], inputs[1], inputs[2], inputs[3], carried_state)
        return (carried_state, outputs)
    initial = jnp.zeros((head_count, HEAD, HEAD), jnp.float32)
    _, outputs = lax.scan(advance, initial, (blocked(lin_query), blocked(lin_key), blocked(lin_value), decays))
    return normalize(outputs.reshape(row_total, head_count, HEAD), norm_gain)

def softmax_layer(queries, span_keys, span_values, cache_keys, cache_values, cache_valid):
    group_size = HEADS // KV_HEADS
    all_keys = jnp.concatenate([cache_keys, span_keys], axis=0)
    all_values = jnp.concatenate([cache_values, span_values], axis=0)
    slot_count = cache_keys.shape[0]
    query_rows = math.gcd(SPAN, 512)

    def per_head(head_index):
        head_keys = lax.dynamic_index_in_dim(all_keys, head_index, 1, False).astype(jnp.float32)
        head_values = lax.dynamic_index_in_dim(all_values, head_index, 1, False).astype(jnp.float32)
        head_queries = lax.dynamic_slice_in_dim(queries, head_index * group_size, group_size, 1)

        def per_block(row_start):
            query_block = lax.dynamic_slice_in_dim(head_queries, row_start, query_rows, 0).astype(jnp.float32)
            scores = jnp.einsum('tgd,ud->gtu', query_block, head_keys) * score_scale
            query_index = row_start + jnp.arange(query_rows, dtype=jnp.int32)
            key_index = jnp.arange(SPAN, dtype=jnp.int32)
            visible = jnp.concatenate([jnp.broadcast_to(cache_valid[None, :], (query_rows, slot_count)), query_index[:, None] >= key_index[None, :]], axis=1)
            row_peak = lax.optimization_barrier(jnp.max(jnp.where(visible[None], scores, -1e+30), axis=-1))
            weights = jnp.where(visible[None], jnp.exp(scores - row_peak[..., None]), 0.0)
            weight_sum = lax.optimization_barrier(jnp.sum(weights, axis=-1))
            rounded = weights.astype(jnp.bfloat16)
            weighted = jnp.einsum('gtu,ud->gtd', rounded.astype(jnp.float32), head_values)
            return weighted / weight_sum[..., None]
        row_starts = jnp.arange(SPAN // query_rows, dtype=jnp.int32) * query_rows
        return lax.map(per_block, row_starts)
    result = lax.map(per_head, jnp.arange(KV_HEADS, dtype=jnp.int32))
    return result.transpose(1, 3, 0, 2, 4).reshape(SPAN, HEADS * HEAD).astype(jnp.bfloat16)

def reference(lin_query, lin_key, lin_value, log_decay, norm_gain, soft_query, span_kv, cache_kv, cache_lens, span_start):
    linear_out = lightning(lin_query, lin_key, lin_value, log_decay, norm_gain)
    positions = (span_start[0] + jnp.arange(SPAN, dtype=jnp.int32)).astype(jnp.float32)
    combined = soft_query.astype(jnp.float32) + linear_out.astype(jnp.float32)
    queries = rotate(combined.reshape(SPAN, HEADS, HEAD), positions).astype(jnp.bfloat16)
    span_keys = rotate(span_kv[:, 0].astype(jnp.float32), positions).astype(jnp.bfloat16)
    slot_index = jnp.arange(N_BLK * CAP, dtype=jnp.int32)
    slot_limit = cache_lens[slot_index // CAP]
    cache_valid = slot_index % CAP < slot_limit
    attended = softmax_layer(queries, span_keys, span_kv[:, 1], cache_kv[:, 0], cache_kv[:, 1], cache_valid)
    return (linear_out, attended)
```

```python
import math

import jax
import jax.numpy as jnp
import numpy as np
from jax import lax
from jax.experimental import pallas as pl
from jax.experimental.pallas import tpu as pltpu
from jax.sharding import PartitionSpec as P

MESH = pl.DeviceIdType.MESH
BF = jnp.bfloat16
F32 = jnp.float32
EPS = 1e-06
SCALE = np.float32(1.4426950408889634 / math.sqrt(128.0))
RATES = (10000000.0 ** (-np.arange(32) / 32.0)).astype(np.float32)
NEG = -1e30

T = 128
HEADS = 8
ROWS = HEADS * T
CHUNK = 2048
RB = 256
NX, NZ = 4, 8
GROUPS = 16


def nt_dot(a, b):
    return lax.dot_general(a, b, (((1,), (1,)), ((), ())), preferred_element_type=F32)


def dot(a, b):
    return jnp.dot(a, b, preferred_element_type=F32)


def split2(value):
    high = value.astype(BF)
    return high, (value - high.astype(F32)).astype(BF)


class Copies:
    def __init__(self, send_sem, recv_sem):
        self.send_sem, self.recv_sem = send_sem, recv_sem
        self.made = []

    def make(self, src, dst, to):
        number = len(self.made)
        copy = pltpu.make_async_remote_copy(
            src_ref=src,
            dst_ref=dst,
            send_sem=self.send_sem.at[number],
            recv_sem=self.recv_sem.at[number],
            device_id=to,
            device_id_type=MESH,
        )
        self.made.append(copy)
        return copy

    def start(self, src, dst, to):
        copy = self.make(src, dst, to)
        copy.start()
        return copy

    def finish(self):
        for copy in self.made:
            copy.wait_send()


N_COPIES = 80


def kernel(
    lq_hbm,
    lk_hbm,
    lv_hbm,
    ld_ref,
    gain_ref,
    sq_hbm,
    skv_hbm,
    cache_hbm,
    rates_ref,
    lens_ref,
    start_ref,
    lout_ref,
    att_ref,
    lq,
    lk,
    lv,
    sq,
    skv,
    ks,
    vs,
    within,
    expcol,
    lsend,
    lrecv,
    tsend,
    trecv,
    psend,
    precv,
    ssend,
    srecv,
    qown,
    qpar,
    qhl,
    bias,
    m_ref,
    acc_ref,
    s_buf,
    part_out,
    part_stat,
    part_out_in,
    part_stat_in,
    lsem,
    ssem,
    rsem,
    tssem,
    trsem,
    pssem,
    prsem,
    xsem,
    xrsem,
):
    seq, blk = lax.axis_index("seq"), lax.axis_index("blk")
    x = lax.rem(seq, NX)
    group = seq // NX
    z = lax.rem(group, NZ)
    yh = group // NZ
    yl, core = blk // 2, lax.rem(blk, 2)

    def at(yh_, z_, x_, blk_):
        return ((yh_ * NZ + z_) * NX + x_, blk_)

    def x_peer(d):
        return at(yh, z, lax.rem(x + d, NX), blk)

    def group_of(g):
        return (g * NX + x, blk)

    z_up, z_down = lax.rem(z + 1, NZ), lax.rem(z + NZ - 1, NZ)
    up, down = at(yh, z_up, x, blk), at(yh, z_down, x, blk)
    sibling = blk + 1 - 2 * core
    y_partner = at(1 - yh, z, x, blk)

    loads = [
        pltpu.make_async_copy(src, dst, lsem.at[i])
        for i, (src, dst) in enumerate(
            [
                (skv_hbm, skv),
                (lk_hbm, lk),
                (lv_hbm, lv),
                (lq_hbm, lq),
                (sq_hbm, sq),
                (cache_hbm.at[blk, 0], ks.at[pl.ds(8 + 2 * blk, 2)]),
                (cache_hbm.at[blk, 1], vs.at[pl.ds(8 + 2 * blk, 2)]),
            ]
        )
    ]
    for load in loads:
        load.start()

    barrier = pltpu.get_barrier_semaphore()

    def greet(device):
        pl.semaphore_signal(barrier, inc=1, device_id=device, device_id_type=MESH)

    for d in range(1, NX):
        greet(x_peer(d))
    for d in range(1, GROUPS):
        greet(group_of(lax.rem(group + d, GROUPS)))
    greet((seq, sibling))
    for yh_ in range(2):
        for core_ in range(2):
            greet(at(yh_, z, x, (1 - yl) * 2 + core_))
    pl.semaphore_wait(barrier, 23)

    copies = Copies(ssem, rsem)

    loads[0].wait()
    vs[0, x] = skv[1]
    vz, vx, kz = {}, [], {}

    def send_vz(step):
        up_from, up_to = (9 - step) % 8, 8 - step
        down_from, down_to = step - 1, step
        if step < 4:
            vz["u", step] = copies.start(vs.at[up_from, x], vs.at[up_to, x], up)
            vz["d", step] = copies.start(vs.at[down_from, x], vs.at[down_to, x], down)
        else:
            half = T // 2
            first, last = pl.ds(0, half), pl.ds(half, half)
            vz["u", step] = copies.start(vs.at[up_from, x, first], vs.at[up_to, x, first], up)
            vz["d", step] = copies.start(vs.at[down_from, x, last], vs.at[down_to, x, last], down)

    def wait_vz(step):
        vz["u", step].wait_recv()
        vz["d", step].wait_recv()

    def send_vx(slot):
        for d in range(1, NX):
            vx.append(copies.start(vs.at[slot, x], vs.at[slot, x], x_peer(d)))

    def send_kz(step):
        up_from, up_to = (9 - step) % 8, 8 - step
        down_from, down_to = step - 1, step
        if step < 4:
            kz["u", step] = copies.start(ks.at[up_from], ks.at[up_to], up)
            kz["d", step] = copies.start(ks.at[down_from], ks.at[down_to], down)
        else:
            first, last = pl.ds(0, 2), pl.ds(2, 2)
            kz["u", step] = copies.start(ks.at[up_from, first], ks.at[up_to, first], up)
            kz["d", step] = copies.start(ks.at[down_from, last], ks.at[down_to, last], down)

    def wait_kz(step):
        kz["u", step].wait_recv()
        kz["d", step].wait_recv()

    send_vz(1)
    send_vx(0)

    lane = lax.broadcasted_iota(jnp.int32, (T, T), 1)
    row = lax.broadcasted_iota(jnp.int32, (T, T), 0)
    positions = (start_ref[0] + seq * T + row).astype(F32)
    angles = positions * rates_ref[0:1, :]
    sine = jnp.sin(angles)
    cos_t = jnp.where(lane < 64, jnp.cos(angles), 1.0)
    sin_t = jnp.where(lane < 32, -sine, jnp.where(lane < 64, sine, 0.0))

    def rotate(features):
        partner = jnp.where(lane < 32, pltpu.roll(features, 96, 1), pltpu.roll(features, 32, 1))
        return features * cos_t + partner * sin_t

    ks[0, x] = rotate(skv[0].astype(F32)).astype(BF)
    kx = [copies.start(ks.at[0, x], ks.at[0, x], x_peer(d)) for d in range(1, NX)]

    cumulative = ld_ref[...]
    lane8 = lax.broadcasted_iota(jnp.int32, (HEADS, T), 1)
    shift = 1
    while shift < T:
        cumulative = cumulative + jnp.where(lane8 >= shift, pltpu.roll(cumulative, shift, 1), 0.0)
        shift *= 2
    last = cumulative[:, T - 1 : T]
    tail = jnp.exp(last - cumulative)
    decay_high, decay_low = split2(jnp.broadcast_to(jnp.exp(last), (HEADS, T)))
    loads[1].wait()
    loads[2].wait()
    for h in range(HEADS):
        cols = pl.ds(h * T, T)
        keys_t = lk[:, cols].astype(F32).T * tail[h : h + 1, :]
        local = dot(keys_t.astype(BF), lv[:, cols])
        lsend[h // 2, pl.ds((h % 2) * T, T)] = local.astype(BF)
    for pair in range(NX):
        rows_ = [
            jnp.broadcast_to(part[h : h + 1, :].astype(F32), (8, T))
            for h in (2 * pair, 2 * pair + 1)
            for part in (decay_high, decay_low)
        ]
        lsend[pair, pl.ds(2 * T, 32)] = jnp.concatenate(rows_, axis=0).astype(BF)
    lx = [
        copies.start(lsend.at[lax.rem(x + d, NX)], lrecv.at[x], x_peer(d)) for d in range(1, NX)
    ]
    lrecv[x] = lsend[x]

    cache_in = []
    for kv, buf in ((0, ks), (1, vs)):
        cache_in.append(
            copies.start(
                cache_hbm.at[sibling, kv], buf.at[pl.ds(8 + 2 * blk, 2)], (seq, sibling)
            )
        )
        for flip in range(2):
            for swap in range(2):
                yh_ = yh + flip - 2 * flip * yh
                other = (1 - yl) * 2 + core + swap - 2 * swap * core
                cache_in.append(
                    copies.start(
                        cache_hbm.at[other, kv, yh],
                        buf.at[8 + 2 * blk + yh],
                        at(yh_, z, x, other),
                    )
                )

    causal = row >= lane
    loads[3].wait()
    for h in range(HEADS):
        cols = pl.ds(h * T, T)
        across = jnp.broadcast_to(cumulative[h : h + 1, :], (T, T))
        downward = across.T
        weights = jnp.where(causal, jnp.exp(jnp.minimum(downward - across, 0.0)), 0.0)
        scores = nt_dot(lq[:, cols], lk[:, cols])
        within[h] = dot((scores * weights).astype(BF), lv[:, cols])
        expcol[h] = jnp.exp(downward)

    for copy in kx:
        copy.wait_recv()
    send_kz(1)
    wait_vz(1)
    send_vz(2)
    send_vx(7)
    send_vx(1)

    for copy in lx:
        copy.wait_recv()

    def decay_of(i):
        tile = lrecv[i, pl.ds(2 * T, 32)].astype(F32)
        return [tile[0:8] + tile[8:16], tile[16:24] + tile[24:32]]

    def state_rows(i, k):
        return lrecv[i, pl.ds(k * T, T)].astype(F32)

    decays = [decay_of(i) for i in range(NX)]
    tall = [[jnp.concatenate([d_] * 16, axis=0) for d_ in pair] for pair in decays]
    for k in range(2):
        total, overall = state_rows(0, k), decays[0][k]
        for i in range(1, NX):
            total = total * tall[i][k] + state_rows(i, k)
            overall = overall * decays[i][k]
        high, low = split2(overall)
        tail_rows = jnp.concatenate([high.astype(F32), low.astype(F32)], axis=0).astype(BF)
        for i in range(8):
            tsend[8 * k + i, pl.ds(0, 16)] = total[16 * i : 16 * i + 16].astype(BF)
            tsend[8 * k + i, pl.ds(16, 16)] = tail_rows

    def t_copy(d):
        to = lax.rem(group + d, GROUPS)
        return pltpu.make_async_remote_copy(
            src_ref=tsend.at[to],
            dst_ref=trecv.at[group],
            send_sem=tssem.at[d],
            recv_sem=trsem.at[d],
            device_id=group_of(to),
            device_id_type=MESH,
        )

    def p_copy(d):
        to = lax.rem(group + d, GROUPS)
        return pltpu.make_async_remote_copy(
            src_ref=psend.at[to],
            dst_ref=precv.at[group],
            send_sem=pssem.at[d],
            recv_sem=prsem.at[d],
            device_id=group_of(to),
            device_id_type=MESH,
        )

    def each_group(action):
        def one(d, carry):
            action(d)
            return carry

        lax.fori_loop(1, GROUPS, one, 0)

    each_group(lambda d: t_copy(d).start())
    trecv[group] = tsend[group]

    wait_kz(1)
    send_kz(2)
    wait_vz(2)
    send_vz(3)
    send_vx(6)
    send_vx(2)

    each_group(lambda d: t_copy(d).wait_recv())
    state = jnp.zeros((16, T), F32)
    for g in range(GROUPS):
        psend[g] = state.astype(BF)
        if g < GROUPS - 1:
            tile = trecv[g, pl.ds(16, 16)].astype(F32)
            decay = tile[0:8] + tile[8:16]
            state = state * jnp.concatenate([decay, decay], axis=0) + trecv[
                g, pl.ds(0, 16)
            ].astype(F32)
    each_group(lambda d: p_copy(d).start())
    precv[group] = psend[group]

    wait_kz(2)
    send_kz(3)
    wait_vz(3)
    send_vz(4)
    send_vx(5)
    send_vx(3)

    each_group(lambda d: p_copy(d).wait_recv())
    for k in range(2):
        state = precv[pl.ds(8 * k, 8)].astype(F32).reshape(T, T)
        for i in range(NX):
            ssend[i, pl.ds(k * T, T)] = state.astype(BF)
            if i < NX - 1:
                state = state * tall[i][k] + state_rows(i, k)
    sx = [
        copies.start(ssend.at[lax.rem(x + d, NX)], srecv.at[x], x_peer(d)) for d in range(1, NX)
    ]
    srecv[x] = ssend[x]

    wait_kz(3)
    send_kz(4)
    wait_vz(4)
    send_vx(4)

    col = lax.broadcasted_iota(jnp.int32, (8, CHUNK), 1)
    visible_from = 512 * (8 - z)
    bias[0] = jnp.where((col < x * T) | (col >= visible_from), 0.0, NEG)
    bias[1] = jnp.where(col + CHUNK >= visible_from, 0.0, NEG)
    for c in range(2):
        bias[2 + c] = jnp.where(
            ((col < 1024) & (col < lens_ref[2 * c]))
            | ((col >= 1024) & (col - 1024 < lens_ref[2 * c + 1])),
            0.0,
            NEG,
        )
    bias[4] = jnp.zeros((8, CHUNK), F32)

    loads[4].wait()
    for copy in sx:
        copy.wait_recv()
    for h in range(HEADS):
        cols = pl.ds(h * T, T)
        carried = dot(lq[:, cols], srecv[h // 2, pl.ds((h % 2) * T, T)])
        light = within[h] + expcol[h] * carried
        mean = jnp.mean(light * light, axis=1, keepdims=True)
        out = (light * lax.rsqrt(mean + EPS) * gain_ref[h : h + 1, :]).astype(BF)
        lout_ref[:, cols] = out
        query = rotate(sq[:, cols].astype(F32) + out.astype(F32)).astype(BF)
        rows_ = pl.ds(h * T, T)
        qown[rows_, :] = query
        high, low = split2(query.astype(F32) * SCALE)
        qhl[0, rows_, pl.ds(0, T)] = high
        qhl[0, rows_, pl.ds(T, T)] = low

    def q_copy():
        return pltpu.make_async_remote_copy(
            src_ref=qown,
            dst_ref=qpar,
            send_sem=xsem.at[0],
            recv_sem=xrsem.at[0],
            device_id=y_partner,
            device_id_type=MESH,
        )

    def back_copies():
        return [
            pltpu.make_async_remote_copy(
                src_ref=src,
                dst_ref=dst,
                send_sem=xsem.at[1 + i],
                recv_sem=xrsem.at[1 + i],
                device_id=y_partner,
                device_id_type=MESH,
            )
            for i, (src, dst) in enumerate(
                [(part_out, part_out_in), (part_stat, part_stat_in)]
            )
        ]

    @pl.when(yh == 1)
    def _():
        q_copy().start()

    own_k, own_v = ks[0, x], vs[0, x]
    own_k2 = jnp.concatenate([own_k, own_k], axis=1)
    own_v2 = jnp.concatenate([own_v, jnp.ones_like(own_v)], axis=1)
    for h in range(HEADS):
        rows_ = pl.ds(h * T, T)
        scores = jnp.where(causal, nt_dot(qhl[0, rows_, :], own_k2), NEG)
        peak = jnp.broadcast_to(jnp.max(scores, axis=1, keepdims=True), (T, T))
        m_ref[0, rows_, :] = peak
        acc_ref[0, rows_, :] = dot(jnp.exp2(scores - peak).astype(BF), own_v2)

    @pl.when(yh == 0)
    def _():
        m_ref[1] = jnp.full((ROWS, T), NEG, F32)
        acc_ref[1] = jnp.zeros((ROWS, 2 * T), F32)

    wait_kz(4)
    for copy in vx + cache_in:
        copy.wait_recv()
    loads[5].wait()
    loads[6].wait()

    def finish_rows(which, h):
        rows_ = pl.ds(h * T, T)
        return m_ref[which, rows_, :], acc_ref[which, rows_, 0:T], acc_ref[which, rows_, T : 2 * T]

    def job(j, carry):
        early = 1 - yh
        which = early * lax.rem(j // 2, 2)
        chunk = early * (lax.rem(j, 2) + 2 * (j // 4)) + yh * j
        mask = chunk + which * (4 - chunk)

        @pl.when((yh == 0) & (j == 2))
        def _():
            q_copy().wait_recv()
            high, low = split2(qpar[...].astype(F32) * SCALE)
            qhl[1, :, pl.ds(0, T)] = high
            qhl[1, :, pl.ds(T, T)] = low

        keys = ks[pl.ds(4 * chunk, 4)].reshape(CHUNK, T)
        keys2 = jnp.concatenate([keys, keys], axis=1)
        values = vs[pl.ds(4 * chunk, 4)].reshape(CHUNK, T)
        values2 = jnp.concatenate([values, jnp.ones_like(values)], axis=1)
        shade = bias[mask, 0:1, :]
        steps = ROWS // RB
        s_buf[0] = nt_dot(qhl[which, pl.ds(0, RB), :], keys2)
        for r in range(steps):
            rows_ = pl.ds(r * RB, RB)
            if r < steps - 1:
                s_buf[(r + 1) % 2] = nt_dot(qhl[which, pl.ds((r + 1) * RB, RB), :], keys2)
            scores = s_buf[r % 2] + shade
            best = scores[:, 0:T]
            for i in range(1, CHUNK // T):
                best = jnp.maximum(best, scores[:, i * T : (i + 1) * T])
            old = m_ref[which, rows_, :]
            new = jnp.maximum(old, jnp.max(best, axis=1, keepdims=True))
            shrink = jnp.exp2(old - new)
            m_ref[which, rows_, :] = new
            weights = jnp.exp2(scores - jnp.concatenate([new] * (CHUNK // T), axis=1)).astype(BF)
            acc_ref[which, rows_, :] = acc_ref[which, rows_, :] * jnp.concatenate(
                [shrink, shrink], axis=1
            ) + dot(weights, values2)

        @pl.when((yh == 0) & (j == 3))
        def _():
            for h in range(HEADS):
                peak, top, total = finish_rows(1, h)
                part_out[pl.ds(h * T, T), :] = (top / total).astype(BF)
                part_stat[pl.ds(h, 1), :] = (peak + jnp.log2(total)).T[0:1, :]
            for copy in back_copies():
                copy.start()

        return carry

    lax.fori_loop(0, 6 - 2 * yh, job, 0)

    @pl.when(yh == 0)
    def _():
        for h in range(HEADS):
            _, top, total = finish_rows(0, h)
            att_ref[:, pl.ds(h * T, T)] = (top / total).astype(BF)
        for copy in back_copies():
            copy.wait_send()

    @pl.when(yh == 1)
    def _():
        q_copy().wait_send()
        for copy in back_copies():
            copy.wait_recv()
        for h in range(HEADS):
            peak, top, total = finish_rows(0, h)
            other = jnp.broadcast_to(part_stat_in[pl.ds(h, 1), :], (T, T)).T
            best = jnp.maximum(peak, other)
            mine, theirs = jnp.exp2(peak - best), jnp.exp2(other - best)
            merged = top * mine + part_out_in[pl.ds(h * T, T), :].astype(F32) * theirs
            att_ref[:, pl.ds(h * T, T)] = (merged / (total * mine + theirs)).astype(BF)

    each_group(lambda d: t_copy(d).wait_send())
    each_group(lambda d: p_copy(d).wait_send())
    copies.finish()


def per_device(lq, lk, lv, ld, gain, sq, skv, cache, lens, start):
    any_space = pl.BlockSpec(memory_space=pl.ANY)
    vmem = pl.BlockSpec(memory_space=pltpu.VMEM)
    smem = pl.BlockSpec(memory_space=pltpu.SMEM)
    rates = np.zeros((8, T), np.float32)
    rates[:, 0:32] = RATES
    rates[:, 32:64] = RATES
    skv_t = skv.reshape(T, 2, T).transpose(1, 0, 2)
    cache_t = cache.transpose(2, 1, 0, 3).reshape(4, 2, 2, NX, T, T)
    scratch = [
        pltpu.VMEM((T, ROWS), BF),
        pltpu.VMEM((T, ROWS), BF),
        pltpu.VMEM((T, ROWS), BF),
        pltpu.VMEM((T, ROWS), BF),
        pltpu.VMEM((2, T, T), BF),
        pltpu.VMEM((16, NX, T, T), BF),
        pltpu.VMEM((16, NX, T, T), BF),
        pltpu.VMEM((HEADS, T, T), F32),
        pltpu.VMEM((HEADS, T, T), F32),
        pltpu.VMEM((NX, 2 * T + 32, T), BF),
        pltpu.VMEM((NX, 2 * T + 32, T), BF),
        pltpu.VMEM((GROUPS, 32, T), BF),
        pltpu.VMEM((GROUPS, 32, T), BF),
        pltpu.VMEM((GROUPS, 16, T), BF),
        pltpu.VMEM((GROUPS, 16, T), BF),
        pltpu.VMEM((NX, 2 * T, T), BF),
        pltpu.VMEM((NX, 2 * T, T), BF),
        pltpu.VMEM((ROWS, T), BF),
        pltpu.VMEM((ROWS, T), BF),
        pltpu.VMEM((2, ROWS, 2 * T), BF),
        pltpu.VMEM((5, 8, CHUNK), F32),
        pltpu.VMEM((2, ROWS, T), F32),
        pltpu.VMEM((2, ROWS, 2 * T), F32),
        pltpu.VMEM((2, RB, CHUNK), F32),
        pltpu.VMEM((ROWS, T), BF),
        pltpu.VMEM((HEADS, T), F32),
        pltpu.VMEM((ROWS, T), BF),
        pltpu.VMEM((HEADS, T), F32),
        pltpu.SemaphoreType.DMA((7,)),
        pltpu.SemaphoreType.DMA((N_COPIES,)),
        pltpu.SemaphoreType.DMA((N_COPIES,)),
        pltpu.SemaphoreType.DMA((GROUPS,)),
        pltpu.SemaphoreType.DMA((GROUPS,)),
        pltpu.SemaphoreType.DMA((GROUPS,)),
        pltpu.SemaphoreType.DMA((GROUPS,)),
        pltpu.SemaphoreType.DMA((3,)),
        pltpu.SemaphoreType.DMA((3,)),
    ]
    return pl.pallas_call(
        kernel,
        out_shape=(
            jax.ShapeDtypeStruct((T, ROWS), BF),
            jax.ShapeDtypeStruct((T, ROWS), BF),
        ),
        in_specs=[
            any_space,
            any_space,
            any_space,
            vmem,
            vmem,
            any_space,
            any_space,
            any_space,
            vmem,
            smem,
            smem,
        ],
        out_specs=(vmem, vmem),
        scratch_shapes=scratch,
        compiler_params=pltpu.CompilerParams(
            collective_id=0, has_side_effects=True, vmem_limit_bytes=48 * 2**20
        ),
    )(lq, lk, lv, ld, gain.reshape(HEADS, T), sq, skv_t, cache_t, jnp.asarray(rates), lens, start)


def solution(mesh):
    in_specs = (
        P("seq", "blk"),
        P("seq", "blk"),
        P("seq", "blk"),
        P("blk", "seq"),
        P("blk"),
        P("seq", "blk"),
        P("seq", None, "blk", None),
        P("blk", None, None, None),
        P(),
        P(),
    )
    out_specs = (P("seq", "blk"), P("seq", "blk"))
    return jax.shard_map(
        per_device, mesh=mesh, in_specs=in_specs, out_specs=out_specs, check_vma=False
    )
```

```python
import math

import jax
import jax.numpy as jnp
import numpy as np
from jax import lax
from jax.experimental import pallas as pl
from jax.experimental.pallas import tpu as pltpu
from jax.sharding import PartitionSpec as P

MESH = pl.DeviceIdType.MESH
BF = jnp.bfloat16
F32 = jnp.float32
EPS = 1e-06
SCALE = np.float32(1.4426950408889634 / math.sqrt(128.0))
RATES = (10000000.0 ** (-np.arange(32) / 32.0)).astype(np.float32)
NEG = -1e30

T = 128
HEADS = 8
ROWS = HEADS * T
CHUNK = 2048
RB = 256
NX, NZ = 4, 8
QZ = 4
SLICE = 2 * T // QZ
GROUPS = 16


def nt_dot(a, b):
    return lax.dot_general(a, b, (((1,), (1,)), ((), ())), preferred_element_type=F32)


def dot(a, b):
    return jnp.dot(a, b, preferred_element_type=F32)


def split2(value):
    high = value.astype(BF)
    return high, (value - high.astype(F32)).astype(BF)


class Copies:
    def __init__(self, send_sem, recv_sem):
        self.send_sem, self.recv_sem = send_sem, recv_sem
        self.made = []

    def make(self, src, dst, to):
        number = len(self.made)
        copy = pltpu.make_async_remote_copy(
            src_ref=src,
            dst_ref=dst,
            send_sem=self.send_sem.at[number],
            recv_sem=self.recv_sem.at[number],
            device_id=to,
            device_id_type=MESH,
        )
        self.made.append(copy)
        return copy

    def start(self, src, dst, to):
        copy = self.make(src, dst, to)
        copy.start()
        return copy

    def finish(self):
        for copy in self.made:
            copy.wait_send()


N_COPIES = 64


def one_hot(major, minor):
    size = major * minor
    out = lax.broadcasted_iota(jnp.int32, (size, size), 0)
    source = lax.broadcasted_iota(jnp.int32, (size, size), 1)
    wanted = lax.rem(out, minor) * major + out // minor
    return jnp.where(source == wanted, 1.0, 0.0).astype(BF)


def kernel(
    lq_hbm,
    lk_hbm,
    lv_hbm,
    ld_ref,
    gain_ref,
    sq_hbm,
    skv_ref,
    cache_hbm,
    rates_ref,
    lens_ref,
    start_ref,
    lout_ref,
    att_ref,
    lq,
    lk,
    lv,
    sq,
    cache_raw,
    cache,
    ks,
    vs,
    within,
    expcol,
    lsend,
    lrecv,
    tsend,
    trecv,
    psend,
    precv,
    ssend,
    srecv,
    qown,
    qpar,
    qhl,
    bias,
    m_ref,
    acc_ref,
    s_buf,
    part_out,
    part_stat,
    part_out_in,
    part_stat_in,
    lsem,
    ssem,
    rsem,
    tssem,
    trsem,
    pssem,
    prsem,
    xsem,
    xrsem,
    ready,
):
    seq, blk = lax.axis_index("seq"), lax.axis_index("blk")
    x = lax.rem(seq, NX)
    z = lax.rem(seq // NX, NZ)
    yh = seq // (NX * NZ)
    yl, core = blk // 2, lax.rem(blk, 2)

    def at(yh_, z_, x_, blk_):
        return ((yh_ * NZ + z_) * NX + x_, blk_)

    def x_peer(d):
        return at(yh, z, lax.rem(x + d, NX), blk)

    group = yh * NZ + z
    quarter, zq = group // QZ, lax.rem(z, QZ)
    first_group = quarter * QZ

    def quarter_peer(d):
        place = lax.rem(zq * NX + x + d, QZ * NX)
        return place // NX, at(0, first_group + place // NX, lax.rem(place, NX), blk)

    def column(g):
        return at(0, g, x, blk)

    up, down = at(yh, lax.rem(z + 1, NZ), x, blk), at(yh, lax.rem(z + NZ - 1, NZ), x, blk)
    sibling = blk + 1 - 2 * core
    y_partner = at(1 - yh, z, x, blk)

    def each(first, last, action):
        def one(d, carry):
            action(d)
            return carry

        lax.fori_loop(first, last, one, 0)

    barrier = pltpu.get_barrier_semaphore()

    def greet(device):
        pl.semaphore_signal(barrier, inc=1, device_id=device, device_id_type=MESH)

    each(1, QZ * NX, lambda d: greet(quarter_peer(d)[1]))
    greet((seq, sibling))
    for yh_ in range(2):
        for core_ in range(2):
            greet(at(yh_, z, x, (1 - yl) * 2 + core_))
    each(first_group + QZ, GROUPS, lambda g: greet(column(g)))

    loads = [
        pltpu.make_async_copy(src, dst, lsem.at[i])
        for i, (src, dst) in enumerate(
            [(lk_hbm, lk), (lv_hbm, lv), (lq_hbm, lq), (sq_hbm, sq), (cache_hbm, cache_raw)]
        )
    ]
    for load in loads:
        load.start()

    cumulative = ld_ref[...]
    lane8 = lax.broadcasted_iota(jnp.int32, (HEADS, T), 1)
    shift = 1
    while shift < T:
        cumulative = cumulative + jnp.where(lane8 >= shift, pltpu.roll(cumulative, shift, 1), 0.0)
        shift *= 2
    last = cumulative[:, T - 1 : T]
    tail = jnp.exp(last - cumulative)
    decay_high, decay_low = split2(jnp.broadcast_to(jnp.exp(last), (HEADS, T)))
    loads[0].wait()
    loads[1].wait()
    for h in range(HEADS):
        cols = pl.ds(h * T, T)
        keys_t = lk[:, cols].astype(F32).T * tail[h : h + 1, :]
        local = dot(keys_t.astype(BF), lv[:, cols])
        lsend[h // 2, pl.ds((h % 2) * T, T)] = local.astype(BF)
    for pair in range(NX):
        rows_ = [
            jnp.broadcast_to(part[h : h + 1, :].astype(F32), (8, T))
            for h in (2 * pair, 2 * pair + 1)
            for part in (decay_high, decay_low)
        ]
        lsend[pair, pl.ds(2 * T, 32)] = jnp.concatenate(rows_, axis=0).astype(BF)
    lrecv[x] = lsend[x]

    lane = lax.broadcasted_iota(jnp.int32, (T, T), 1)
    row = lax.broadcasted_iota(jnp.int32, (T, T), 0)
    positions = (start_ref[0] + seq * T + row).astype(F32)
    angles = positions * rates_ref[0:1, :]
    sine = jnp.sin(angles)
    cos_t = jnp.where(lane < 64, jnp.cos(angles), 1.0)
    sin_t = jnp.where(lane < 32, -sine, jnp.where(lane < 64, sine, 0.0))

    def rotate(features):
        partner = jnp.where(lane < 32, pltpu.roll(features, 96, 1), pltpu.roll(features, 32, 1))
        return features * cos_t + partner * sin_t

    span = dot(one_hot(2, T), skv_ref[...])
    ks[0, x] = rotate(span[0:T]).astype(BF)
    vs[0, x] = span[T : 2 * T].astype(BF)

    pl.semaphore_wait(barrier, QZ * NX - 1 + 5 + first_group)
    each(
        0,
        first_group,
        lambda g: pl.semaphore_signal(ready, inc=1, device_id=column(g), device_id_type=MESH),
    )

    copies = Copies(ssem, rsem)
    lx = [
        copies.start(lsend.at[lax.rem(x + d, NX)], lrecv.at[x], x_peer(d)) for d in range(1, NX)
    ]

    vz, vx, kz = {}, [], {}

    def send_vz(step):
        if step < 4:
            vz["u", step] = copies.start(vs.at[step - 1, x], vs.at[step, x], up)
            vz["d", step] = copies.start(vs.at[(9 - step) % 8, x], vs.at[8 - step, x], down)
        else:
            first, last_ = pl.ds(0, T // 2), pl.ds(T // 2, T // 2)
            vz["u", step] = copies.start(vs.at[3, x, first], vs.at[4, x, first], up)
            vz["d", step] = copies.start(vs.at[5, x, last_], vs.at[4, x, last_], down)

    def wait_vz(step):
        vz["u", step].wait_recv()
        vz["d", step].wait_recv()

    def send_vx(slot):
        for d in range(1, NX):
            vx.append(copies.start(vs.at[slot, x], vs.at[slot, x], x_peer(d)))

    def send_kz(step):
        if step < 4:
            kz["u", step] = copies.start(ks.at[step - 1], ks.at[step], up)
            kz["d", step] = copies.start(ks.at[(9 - step) % 8], ks.at[8 - step], down)
        else:
            first, last_ = pl.ds(0, 2), pl.ds(2, 2)
            kz["u", step] = copies.start(ks.at[3, first], ks.at[4, first], up)
            kz["d", step] = copies.start(ks.at[5, last_], ks.at[4, last_], down)

    def wait_kz(step):
        kz["u", step].wait_recv()
        kz["d", step].wait_recv()

    kx = [copies.start(ks.at[0, x], ks.at[0, x], x_peer(d)) for d in range(1, NX)]

    causal = row >= lane
    loads[2].wait()
    for h in range(HEADS):
        cols = pl.ds(h * T, T)
        across = jnp.broadcast_to(cumulative[h : h + 1, :], (T, T))
        downward = across.T
        weights = jnp.where(causal, jnp.exp(jnp.minimum(downward - across, 0.0)), 0.0)
        scores = nt_dot(lq[:, cols], lk[:, cols])
        within[h] = dot((scores * weights).astype(BF), lv[:, cols])
        expcol[h] = jnp.exp(downward)

    for copy in lx:
        copy.wait_recv()

    def decay_of(tile):
        wide = tile.astype(F32)
        return [wide[0:8] + wide[8:16], wide[16:24] + wide[24:32]]

    def tall(decay, rows_):
        return jnp.concatenate([decay] * (rows_ // 8), axis=0)

    def two_parts(decay):
        high, low = split2(decay)
        return [high.astype(F32), low.astype(F32)]

    decays = [decay_of(lrecv[i, pl.ds(2 * T, 32)]) for i in range(NX)]
    ones8 = jnp.ones((8, T), F32)
    overall = [ones8, ones8]
    totals = [jnp.zeros((T, T), F32)] * 2
    for i in range(NX):
        for k in range(2):
            ssend[i, pl.ds(k * T, T)] = totals[k].astype(BF)
            totals[k] = totals[k] * tall(decays[i][k], T) + lrecv[i, pl.ds(k * T, T)].astype(F32)
        ssend[i, pl.ds(2 * T, 32)] = jnp.concatenate(
            two_parts(overall[0]) + two_parts(overall[1]), axis=0
        ).astype(BF)
        overall = [overall[k] * decays[i][k] for k in range(2)]
    for k in range(2):
        tail_rows = jnp.concatenate(two_parts(overall[k]), axis=0).astype(BF)
        for i in range(QZ // 2):
            piece = totals[k][SLICE * i : SLICE * (i + 1)]
            tsend[QZ // 2 * k + i, pl.ds(0, SLICE)] = piece.astype(BF)
            tsend[QZ // 2 * k + i, pl.ds(SLICE, 16)] = tail_rows

    def t_copy(g):
        return pltpu.make_async_remote_copy(
            src_ref=tsend.at[lax.rem(g, QZ)],
            dst_ref=trecv.at[group],
            send_sem=tssem.at[g],
            recv_sem=trsem.at[group],
            device_id=column(g),
            device_id_type=MESH,
        )

    def t_arrival(g):
        return pltpu.make_async_remote_copy(
            src_ref=tsend.at[0],
            dst_ref=trecv.at[g],
            send_sem=tssem.at[g],
            recv_sem=trsem.at[g],
            device_id=column(g),
            device_id_type=MESH,
        )

    def quarter_group(d):
        return first_group + lax.rem(zq + d, QZ)

    each(1, QZ, lambda d: t_copy(quarter_group(d)).start())
    trecv[group] = tsend[zq]
    sx = [
        copies.start(ssend.at[lax.rem(x + d, NX)], srecv.at[x], x_peer(d)) for d in range(1, NX)
    ]
    srecv[x] = ssend[x]

    @pl.when(quarter < 3)
    def _():
        pl.semaphore_wait(ready, GROUPS - QZ - first_group)

    each(first_group + QZ, GROUPS, lambda g: t_copy(g).start())
    send_vz(1)
    send_vx(0)
    for copy in kx:
        copy.wait_recv()
    send_kz(1)

    loads[4].wait()
    sort = one_hot(8, 32)

    def relayout(b, carry):
        part = dot(sort, cache_raw[pl.ds(pl.multiple_of(b * 256, 256), 256), :]).astype(BF)
        rows_ = pl.ds(pl.multiple_of(lax.rem(b, 4) * 32, 32), 32)
        for kv in range(2):
            for h in range(4):
                at_ = (kv * 4 + h) * 32
                cache[h, kv, b // 16, lax.rem(b // 4, 4), rows_] = part[at_ : at_ + 32]
        return carry

    lax.fori_loop(0, 32, relayout, 0, unroll=4)

    cache_in = []
    for kv, buf in ((0, ks), (1, vs)):
        cache_in.append(
            copies.start(cache.at[sibling, kv], buf.at[pl.ds(8 + 2 * blk, 2)], (seq, sibling))
        )
        for flip in range(2):
            for swap in range(2):
                yh_ = yh + flip - 2 * flip * yh
                other = (1 - yl) * 2 + core + swap - 2 * swap * core
                cache_in.append(
                    copies.start(
                        cache.at[other, kv, yh],
                        buf.at[8 + 2 * blk + yh],
                        at(yh_, z, x, other),
                    )
                )
        buf[pl.ds(8 + 2 * blk, 2)] = cache[blk, kv]

    wait_vz(1)
    send_vz(2)
    wait_kz(1)
    send_kz(2)

    def chain(g, state):
        tile = trecv[g, pl.ds(SLICE, 16)].astype(F32)
        return state * tall(tile[0:8] + tile[8:16], SLICE) + trecv[g, pl.ds(0, SLICE)].astype(F32)

    def earlier(g, state):
        t_arrival(g).wait_recv()
        return chain(g, state)

    each(1, QZ, lambda d: t_arrival(quarter_group(d)).wait_recv())
    state = lax.fori_loop(0, first_group, earlier, jnp.zeros((SLICE, T), F32))
    for i in range(QZ):
        psend[i] = state.astype(BF)
        if i < QZ - 1:
            state = chain(first_group + i, state)

    def p_copy(d):
        z_, device = quarter_peer(d)
        return pltpu.make_async_remote_copy(
            src_ref=psend.at[z_],
            dst_ref=precv.at[x, zq],
            send_sem=pssem.at[d],
            recv_sem=prsem.at[d],
            device_id=device,
            device_id_type=MESH,
        )

    each(1, QZ * NX, lambda d: p_copy(d).start())
    precv[x, zq] = psend[zq]

    wait_vz(2)
    send_vz(3)
    send_vx(1)
    send_vx(7)
    wait_kz(2)
    send_kz(3)

    col = lax.broadcasted_iota(jnp.int32, (8, CHUNK), 1)
    visible_to = 512 * (z + 1)
    bias[0] = jnp.where((col < x * T) | ((col >= 512) & (col < visible_to)), 0.0, NEG)
    bias[1] = jnp.where(col + CHUNK < visible_to, 0.0, NEG)
    for c in range(2):
        bias[2 + c] = jnp.where(
            ((col < 1024) & (col < lens_ref[2 * c]))
            | ((col >= 1024) & (col - 1024 < lens_ref[2 * c + 1])),
            0.0,
            NEG,
        )
    bias[4] = jnp.zeros((8, CHUNK), F32)

    wait_vz(3)
    send_vz(4)
    send_vx(2)
    send_vx(6)

    for copy in sx:
        copy.wait_recv()
    loads[3].wait()
    each(1, QZ * NX, lambda d: p_copy(d).wait_recv())

    def q_copy(h):
        rows_ = pl.ds(h * T, T)
        return pltpu.make_async_remote_copy(
            src_ref=qown.at[rows_],
            dst_ref=qpar.at[rows_],
            send_sem=xsem.at[2 + h],
            recv_sem=xrsem.at[2 + h],
            device_id=y_partner,
            device_id_type=MESH,
        )

    def back_copies():
        return [
            pltpu.make_async_remote_copy(
                src_ref=src,
                dst_ref=dst,
                send_sem=xsem.at[i],
                recv_sem=xrsem.at[i],
                device_id=y_partner,
                device_id_type=MESH,
            )
            for i, (src, dst) in enumerate(
                [(part_out, part_out_in), (part_stat, part_stat_in)]
            )
        ]

    for h in range(HEADS):
        cols, rows_ = pl.ds(h * T, T), pl.ds(h * T, T)
        pair, k = h // 2, h % 2
        before = precv[pair, pl.ds(QZ // 2 * k, QZ // 2)].reshape(T, T).astype(F32)
        tile = decay_of(srecv[pair, pl.ds(2 * T, 32)])[k]
        state = before * tall(tile, T) + srecv[pair, pl.ds(k * T, T)].astype(F32)
        carried = dot(lq[:, cols], state.astype(BF))
        light = within[h] + expcol[h] * carried
        mean = jnp.mean(light * light, axis=1, keepdims=True)
        out = (light * lax.rsqrt(mean + EPS) * gain_ref[h : h + 1, :]).astype(BF)
        lout_ref[:, cols] = out
        query = rotate(sq[:, cols].astype(F32) + out.astype(F32)).astype(BF)
        qown[rows_, :] = query
        high, low = split2(query.astype(F32) * SCALE)
        qhl[0, rows_, pl.ds(0, T)] = high
        qhl[0, rows_, pl.ds(T, T)] = low

    @pl.when(yh == 1)
    def _():
        each(0, HEADS, lambda h: q_copy(h).start())

    own_k, own_v = ks[0, x], vs[0, x]
    own_k2 = jnp.concatenate([own_k, own_k], axis=1)
    own_v2 = jnp.concatenate([own_v, jnp.ones_like(own_v)], axis=1)
    for h in range(HEADS):
        rows_ = pl.ds(h * T, T)
        scores = jnp.where(causal, nt_dot(qhl[0, rows_, :], own_k2), NEG)
        peak = jnp.broadcast_to(jnp.max(scores, axis=1, keepdims=True), (T, T))
        m_ref[0, rows_, :] = peak
        acc_ref[0, rows_, :] = dot(jnp.exp2(scores - peak).astype(BF), own_v2)

    @pl.when(yh == 0)
    def _():
        m_ref[1] = jnp.full((ROWS, T), NEG, F32)
        acc_ref[1] = jnp.zeros((ROWS, 2 * T), F32)

    wait_kz(3)
    send_kz(4)
    wait_vz(4)
    send_vx(3)
    send_vx(5)
    send_vx(4)
    for copy in cache_in:
        copy.wait_recv()

    def finish_rows(which, h):
        rows_ = pl.ds(h * T, T)
        return m_ref[which, rows_, :], acc_ref[which, rows_, 0:T], acc_ref[which, rows_, T : 2 * T]

    late = z // 4

    def job(v, carry):
        which = (1 - yh) * lax.rem(v // 2, 2)
        chunk = lax.rem(v, 2) + 2 * ((5 - v) // 4)
        mask = chunk + which * (4 - chunk)

        @pl.when(v == 2)
        def _():
            wait_kz(4)
            for copy in vx:
                copy.wait_recv()

        @pl.when((yh == 0) & (v == 2))
        def _():
            each(0, HEADS, lambda h: q_copy(h).wait_recv())
            high, low = split2(qpar[...].astype(F32) * SCALE)
            qhl[1, :, pl.ds(0, T)] = high
            qhl[1, :, pl.ds(T, T)] = low

        keys = ks[pl.ds(4 * chunk, 4)].reshape(CHUNK, T)
        keys2 = jnp.concatenate([keys, keys], axis=1)
        values = vs[pl.ds(4 * chunk, 4)].reshape(CHUNK, T)
        values2 = jnp.concatenate([values, jnp.ones_like(values)], axis=1)
        shade = bias[mask, 0:1, :]
        steps = ROWS // RB
        s_buf[0] = nt_dot(qhl[which, pl.ds(0, RB), :], keys2)
        for r in range(steps):
            rows_ = pl.ds(r * RB, RB)
            if r < steps - 1:
                s_buf[(r + 1) % 2] = nt_dot(qhl[which, pl.ds((r + 1) * RB, RB), :], keys2)
            scores = s_buf[r % 2] + shade
            best = scores[:, 0:T]
            for c in range(1, CHUNK // T):
                best = jnp.maximum(best, scores[:, c * T : (c + 1) * T])
            old = m_ref[which, rows_, :]
            new = jnp.maximum(old, jnp.max(best, axis=1, keepdims=True))
            shrink = jnp.exp2(old - new)
            m_ref[which, rows_, :] = new
            weights = jnp.exp2(scores - jnp.concatenate([new] * (CHUNK // T), axis=1)).astype(BF)
            acc_ref[which, rows_, :] = acc_ref[which, rows_, :] * jnp.concatenate(
                [shrink, shrink], axis=1
            ) + dot(weights, values2)

        @pl.when((yh == 0) & (v == 3))
        def _():
            for h in range(HEADS):
                peak, top, total = finish_rows(1, h)
                part_out[pl.ds(h * T, T), :] = (top / total).astype(BF)
                part_stat[pl.ds(h, 1), :] = (peak + jnp.log2(total)).T[0:1, :]
            for copy in back_copies():
                copy.start()

        return carry

    lax.fori_loop(0, 5 + late - 2 * yh, job, 0)

    @pl.when(yh == 0)
    def _():
        for h in range(HEADS):
            _, top, total = finish_rows(0, h)
            att_ref[:, pl.ds(h * T, T)] = (top / total).astype(BF)
        for copy in back_copies():
            copy.wait_send()

    @pl.when(yh == 1)
    def _():
        each(0, HEADS, lambda h: q_copy(h).wait_send())
        for copy in back_copies():
            copy.wait_recv()
        for h in range(HEADS):
            peak, top, total = finish_rows(0, h)
            other = jnp.broadcast_to(part_stat_in[pl.ds(h, 1), :], (T, T)).T
            best = jnp.maximum(peak, other)
            mine, theirs = jnp.exp2(peak - best), jnp.exp2(other - best)
            merged = top * mine + part_out_in[pl.ds(h * T, T), :].astype(F32) * theirs
            att_ref[:, pl.ds(h * T, T)] = (merged / (total * mine + theirs)).astype(BF)

    each(1, QZ, lambda d: t_copy(quarter_group(d)).wait_send())
    each(first_group + QZ, GROUPS, lambda g: t_copy(g).wait_send())
    each(1, QZ * NX, lambda d: p_copy(d).wait_send())
    copies.finish()


def per_device(lq, lk, lv, ld, gain, sq, skv, cache, lens, start):
    any_space = pl.BlockSpec(memory_space=pl.ANY)
    vmem = pl.BlockSpec(memory_space=pltpu.VMEM)
    smem = pl.BlockSpec(memory_space=pltpu.SMEM)
    rates = np.zeros((8, T), np.float32)
    rates[:, 0:32] = RATES
    rates[:, 32:64] = RATES
    scratch = [
        pltpu.VMEM((T, ROWS), BF),
        pltpu.VMEM((T, ROWS), BF),
        pltpu.VMEM((T, ROWS), BF),
        pltpu.VMEM((T, ROWS), BF),
        pltpu.VMEM((8 * 1024, T), BF),
        pltpu.VMEM((4, 2, 2, NX, T, T), BF),
        pltpu.VMEM((16, NX, T, T), BF),
        pltpu.VMEM((16, NX, T, T), BF),
        pltpu.VMEM((HEADS, T, T), F32),
        pltpu.VMEM((HEADS, T, T), F32),
        pltpu.VMEM((NX, 2 * T + 32, T), BF),
        pltpu.VMEM((NX, 2 * T + 32, T), BF),
        pltpu.VMEM((QZ, SLICE + 16, T), BF),
        pltpu.VMEM((GROUPS, SLICE + 16, T), BF),
        pltpu.VMEM((QZ, SLICE, T), BF),
        pltpu.VMEM((NX, QZ, SLICE, T), BF),
        pltpu.VMEM((NX, 2 * T + 32, T), BF),
        pltpu.VMEM((NX, 2 * T + 32, T), BF),
        pltpu.VMEM((ROWS, T), BF),
        pltpu.VMEM((ROWS, T), BF),
        pltpu.VMEM((2, ROWS, 2 * T), BF),
        pltpu.VMEM((5, 8, CHUNK), F32),
        pltpu.VMEM((2, ROWS, T), F32),
        pltpu.VMEM((2, ROWS, 2 * T), F32),
        pltpu.VMEM((2, RB, CHUNK), F32),
        pltpu.VMEM((ROWS, T), BF),
        pltpu.VMEM((HEADS, T), F32),
        pltpu.VMEM((ROWS, T), BF),
        pltpu.VMEM((HEADS, T), F32),
        pltpu.SemaphoreType.DMA((5,)),
        pltpu.SemaphoreType.DMA((N_COPIES,)),
        pltpu.SemaphoreType.DMA((N_COPIES,)),
        pltpu.SemaphoreType.DMA((GROUPS,)),
        pltpu.SemaphoreType.DMA((GROUPS,)),
        pltpu.SemaphoreType.DMA((QZ * NX,)),
        pltpu.SemaphoreType.DMA((QZ * NX,)),
        pltpu.SemaphoreType.DMA((2 + HEADS,)),
        pltpu.SemaphoreType.DMA((2 + HEADS,)),
        pltpu.SemaphoreType.REGULAR,
    ]
    return pl.pallas_call(
        kernel,
        out_shape=(
            jax.ShapeDtypeStruct((T, ROWS), BF),
            jax.ShapeDtypeStruct((T, ROWS), BF),
        ),
        in_specs=[
            any_space,
            any_space,
            any_space,
            vmem,
            vmem,
            any_space,
            vmem,
            any_space,
            vmem,
            smem,
            smem,
        ],
        out_specs=(vmem, vmem),
        scratch_shapes=scratch,
        compiler_params=pltpu.CompilerParams(
            collective_id=0, has_side_effects=True, vmem_limit_bytes=53 * 2**20
        ),
    )(
        lq,
        lk,
        lv,
        ld,
        gain.reshape(HEADS, T),
        sq,
        skv.reshape(2 * T, T),
        cache.reshape(8 * 1024, T),
        jnp.asarray(rates),
        lens,
        start,
    )


def solution(mesh):
    in_specs = (
        P("seq", "blk"),
        P("seq", "blk"),
        P("seq", "blk"),
        P("blk", "seq"),
        P("blk"),
        P("seq", "blk"),
        P("seq", None, "blk", None),
        P("blk", None, None, None),
        P(),
        P(),
    )
    out_specs = (P("seq", "blk"), P("seq", "blk"))
    return jax.shard_map(
        per_device, mesh=mesh, in_specs=in_specs, out_specs=out_specs, check_vma=False
    )
```

```python
import math

import jax
import jax.numpy as jnp
import numpy as np
from jax import lax
from jax.experimental import pallas as pl
from jax.experimental.pallas import tpu as pltpu
from jax.sharding import PartitionSpec as P

MESH = pl.DeviceIdType.MESH
BF = jnp.bfloat16
F32 = jnp.float32
EPS = 1e-06
SCALE = np.float32(1.4426950408889634 / math.sqrt(128.0))
RATES = (10000000.0 ** (-np.arange(32) / 32.0)).astype(np.float32)
NEG = -1e30

T = 128
HEADS = 8
ROWS = HEADS * T
CHUNK = 2048
RB = 256
NX, NZ = 4, 8
QZ = 4
SLICE = 2 * T // QZ
GROUPS = 16


def nt_dot(a, b):
    return lax.dot_general(a, b, (((1,), (1,)), ((), ())), preferred_element_type=F32)


def dot(a, b):
    return jnp.dot(a, b, preferred_element_type=F32)


def split2(value):
    high = value.astype(BF)
    return high, (value - high.astype(F32)).astype(BF)


class Copies:
    def __init__(self, send_sem, recv_sem):
        self.send_sem, self.recv_sem = send_sem, recv_sem
        self.made = []

    def make(self, src, dst, to):
        number = len(self.made)
        copy = pltpu.make_async_remote_copy(
            src_ref=src,
            dst_ref=dst,
            send_sem=self.send_sem.at[number],
            recv_sem=self.recv_sem.at[number],
            device_id=to,
            device_id_type=MESH,
        )
        self.made.append(copy)
        return copy

    def start(self, src, dst, to):
        copy = self.make(src, dst, to)
        copy.start()
        return copy

    def finish(self):
        for copy in self.made:
            copy.wait_send()


N_COPIES = 64


def one_hot(major, minor):
    size = major * minor
    out = lax.broadcasted_iota(jnp.int32, (size, size), 0)
    source = lax.broadcasted_iota(jnp.int32, (size, size), 1)
    wanted = lax.rem(out, minor) * major + out // minor
    return jnp.where(source == wanted, 1.0, 0.0).astype(BF)


def kernel(
    lq_hbm,
    lk_hbm,
    lv_hbm,
    ld_hbm,
    gain_hbm,
    sq_hbm,
    skv_hbm,
    cache_hbm,
    rates_hbm,
    lens_ref,
    start_ref,
    lout_ref,
    att_ref,
    lq,
    lk,
    lv,
    sq,
    cache_raw,
    cache,
    ks,
    vs,
    within,
    expcol,
    lsend,
    lrecv,
    tsend,
    trecv,
    psend,
    precv,
    ssend,
    srecv,
    qown,
    qpar,
    qhl,
    bias,
    m_ref,
    acc_ref,
    s_buf,
    part_out,
    part_stat,
    part_out_in,
    part_stat_in,
    lout,
    att,
    ld,
    skv,
    gain,
    rates,
    lsem,
    ssem,
    rsem,
    tssem,
    trsem,
    pssem,
    prsem,
    xsem,
    xrsem,
    ready,
):
    seq, blk = lax.axis_index("seq"), lax.axis_index("blk")
    x = lax.rem(seq, NX)
    z = lax.rem(seq // NX, NZ)
    yh = seq // (NX * NZ)
    yl, core = blk // 2, lax.rem(blk, 2)

    def at(yh_, z_, x_, blk_):
        return ((yh_ * NZ + z_) * NX + x_, blk_)

    def x_peer(d):
        return at(yh, z, lax.rem(x + d, NX), blk)

    group = yh * NZ + z
    quarter, zq = group // QZ, lax.rem(z, QZ)
    first_group = quarter * QZ

    def quarter_peer(d):
        place = lax.rem(zq * NX + x + d, QZ * NX)
        return place // NX, at(0, first_group + place // NX, lax.rem(place, NX), blk)

    def column(g):
        return at(0, g, x, blk)

    up, down = at(yh, lax.rem(z + 1, NZ), x, blk), at(yh, lax.rem(z + NZ - 1, NZ), x, blk)
    sibling = blk + 1 - 2 * core
    y_partner = at(1 - yh, z, x, blk)

    def each(first, last, action):
        def one(d, carry):
            action(d)
            return carry

        lax.fori_loop(first, last, one, 0)

    loads = [
        pltpu.make_async_copy(src, dst, lsem.at[i])
        for i, (src, dst) in enumerate(
            [
                (lk_hbm, lk),
                (lv_hbm, lv),
                (lq_hbm, lq),
                (sq_hbm, sq),
                (cache_hbm, cache_raw),
                (ld_hbm, ld),
                (skv_hbm, skv),
                (gain_hbm, gain),
                (rates_hbm, rates),
            ]
        )
    ]
    for i in (5, 0, 1, 6, 8, 2, 4, 3, 7):
        loads[i].start()

    barrier = pltpu.get_barrier_semaphore()

    def greet(device):
        pl.semaphore_signal(barrier, inc=1, device_id=device, device_id_type=MESH)

    each(1, QZ * NX, lambda d: greet(quarter_peer(d)[1]))
    greet((seq, sibling))
    for yh_ in range(2):
        for core_ in range(2):
            greet(at(yh_, z, x, (1 - yl) * 2 + core_))
    each(first_group + QZ, GROUPS, lambda g: greet(column(g)))

    loads[5].wait()
    cumulative = ld[...]
    lane8 = lax.broadcasted_iota(jnp.int32, (HEADS, T), 1)
    shift = 1
    while shift < T:
        cumulative = cumulative + jnp.where(lane8 >= shift, pltpu.roll(cumulative, shift, 1), 0.0)
        shift *= 2
    last = cumulative[:, T - 1 : T]
    tail = jnp.exp(last - cumulative)
    decay_high, decay_low = split2(jnp.broadcast_to(jnp.exp(last), (HEADS, T)))
    loads[0].wait()
    loads[1].wait()
    for h in range(HEADS):
        cols = pl.ds(h * T, T)
        keys_t = lk[:, cols].astype(F32).T * tail[h : h + 1, :]
        local = dot(keys_t.astype(BF), lv[:, cols])
        lsend[h // 2, pl.ds((h % 2) * T, T)] = local.astype(BF)
    for pair in range(NX):
        rows_ = [
            jnp.broadcast_to(part[h : h + 1, :].astype(F32), (8, T))
            for h in (2 * pair, 2 * pair + 1)
            for part in (decay_high, decay_low)
        ]
        lsend[pair, pl.ds(2 * T, 32)] = jnp.concatenate(rows_, axis=0).astype(BF)
    lrecv[x] = lsend[x]

    pl.semaphore_wait(barrier, QZ * NX - 1 + 5 + first_group)
    each(
        0,
        first_group,
        lambda g: pl.semaphore_signal(ready, inc=1, device_id=column(g), device_id_type=MESH),
    )

    copies = Copies(ssem, rsem)
    lx = [
        copies.start(lsend.at[lax.rem(x + d, NX)], lrecv.at[x], x_peer(d)) for d in range(1, NX)
    ]

    lane = lax.broadcasted_iota(jnp.int32, (T, T), 1)
    row = lax.broadcasted_iota(jnp.int32, (T, T), 0)
    loads[8].wait()
    loads[6].wait()
    positions = (start_ref[0] + seq * T + row).astype(F32)
    angles = positions * rates[0:1, :]
    sine = jnp.sin(angles)
    cos_t = jnp.where(lane < 64, jnp.cos(angles), 1.0)
    sin_t = jnp.where(lane < 32, -sine, jnp.where(lane < 64, sine, 0.0))

    def rotate(features):
        partner = jnp.where(lane < 32, pltpu.roll(features, 96, 1), pltpu.roll(features, 32, 1))
        return features * cos_t + partner * sin_t

    span = dot(one_hot(2, T), skv[...])
    ks[0, x] = rotate(span[0:T]).astype(BF)
    vs[0, x] = span[T : 2 * T].astype(BF)

    vz, vx, kz = {}, [], {}

    def send_vz(step):
        if step < 4:
            vz["u", step] = copies.start(vs.at[step - 1, x], vs.at[step, x], up)
            vz["d", step] = copies.start(vs.at[(9 - step) % 8, x], vs.at[8 - step, x], down)
        else:
            first, last_ = pl.ds(0, T // 2), pl.ds(T // 2, T // 2)
            vz["u", step] = copies.start(vs.at[3, x, first], vs.at[4, x, first], up)
            vz["d", step] = copies.start(vs.at[5, x, last_], vs.at[4, x, last_], down)

    def wait_vz(step):
        vz["u", step].wait_recv()
        vz["d", step].wait_recv()

    def send_vx(slot):
        for d in range(1, NX):
            vx.append(copies.start(vs.at[slot, x], vs.at[slot, x], x_peer(d)))

    def send_kz(step):
        if step < 4:
            kz["u", step] = copies.start(ks.at[step - 1], ks.at[step], up)
            kz["d", step] = copies.start(ks.at[(9 - step) % 8], ks.at[8 - step], down)
        else:
            first, last_ = pl.ds(0, 2), pl.ds(2, 2)
            kz["u", step] = copies.start(ks.at[3, first], ks.at[4, first], up)
            kz["d", step] = copies.start(ks.at[5, last_], ks.at[4, last_], down)

    def wait_kz(step):
        kz["u", step].wait_recv()
        kz["d", step].wait_recv()

    kx = [copies.start(ks.at[0, x], ks.at[0, x], x_peer(d)) for d in range(1, NX)]

    causal = row >= lane
    loads[2].wait()
    for h in range(HEADS):
        cols = pl.ds(h * T, T)
        across = jnp.broadcast_to(cumulative[h : h + 1, :], (T, T))
        downward = across.T
        weights = jnp.where(causal, jnp.exp(jnp.minimum(downward - across, 0.0)), 0.0)
        scores = nt_dot(lq[:, cols], lk[:, cols])
        within[h] = dot((scores * weights).astype(BF), lv[:, cols])
        expcol[h] = jnp.exp(downward)

    @pl.when(quarter < 3)
    def _():
        pl.semaphore_wait(ready, GROUPS - QZ - first_group)

    send_vz(1)
    send_vx(0)
    for copy in kx:
        copy.wait_recv()
    send_kz(1)

    for copy in lx:
        copy.wait_recv()

    def decay_of(tile):
        wide = tile.astype(F32)
        return [wide[0:8] + wide[8:16], wide[16:24] + wide[24:32]]

    def tall(decay, rows_):
        return jnp.concatenate([decay] * (rows_ // 8), axis=0)

    def two_parts(decay):
        high, low = split2(decay)
        return [high.astype(F32), low.astype(F32)]

    decays = [decay_of(lrecv[i, pl.ds(2 * T, 32)]) for i in range(NX)]
    ones8 = jnp.ones((8, T), F32)
    overall = [ones8, ones8]
    totals = [jnp.zeros((T, T), F32)] * 2
    for i in range(NX):
        for k in range(2):
            ssend[i, pl.ds(k * T, T)] = totals[k].astype(BF)
            totals[k] = totals[k] * tall(decays[i][k], T) + lrecv[i, pl.ds(k * T, T)].astype(F32)
        ssend[i, pl.ds(2 * T, 32)] = jnp.concatenate(
            two_parts(overall[0]) + two_parts(overall[1]), axis=0
        ).astype(BF)
        overall = [overall[k] * decays[i][k] for k in range(2)]
    for k in range(2):
        tail_rows = jnp.concatenate(two_parts(overall[k]), axis=0).astype(BF)
        for i in range(QZ // 2):
            piece = totals[k][SLICE * i : SLICE * (i + 1)]
            tsend[QZ // 2 * k + i, pl.ds(0, SLICE)] = piece.astype(BF)
            tsend[QZ // 2 * k + i, pl.ds(SLICE, 16)] = tail_rows

    def t_copy(g):
        return pltpu.make_async_remote_copy(
            src_ref=tsend.at[lax.rem(g, QZ)],
            dst_ref=trecv.at[group],
            send_sem=tssem.at[g],
            recv_sem=trsem.at[group],
            device_id=column(g),
            device_id_type=MESH,
        )

    def t_arrival(g):
        return pltpu.make_async_remote_copy(
            src_ref=tsend.at[0],
            dst_ref=trecv.at[g],
            send_sem=tssem.at[g],
            recv_sem=trsem.at[g],
            device_id=column(g),
            device_id_type=MESH,
        )

    def quarter_group(d):
        return first_group + lax.rem(zq + d, QZ)

    each(1, QZ, lambda d: t_copy(quarter_group(d)).start())
    each(first_group + QZ, GROUPS, lambda g: t_copy(g).start())
    trecv[group] = tsend[zq]
    sx = [
        copies.start(ssend.at[lax.rem(x + d, NX)], srecv.at[x], x_peer(d)) for d in range(1, NX)
    ]
    srecv[x] = ssend[x]

    loads[4].wait()
    sort = one_hot(8, 32)

    def relayout(b, carry):
        part = dot(sort, cache_raw[pl.ds(pl.multiple_of(b * 256, 256), 256), :]).astype(BF)
        rows_ = pl.ds(pl.multiple_of(lax.rem(b, 4) * 32, 32), 32)
        for kv in range(2):
            for h in range(4):
                at_ = (kv * 4 + h) * 32
                cache[h, kv, b // 16, lax.rem(b // 4, 4), rows_] = part[at_ : at_ + 32]
        return carry

    lax.fori_loop(0, 32, relayout, 0, unroll=4)

    cache_in = []
    for kv, buf in ((0, ks), (1, vs)):
        cache_in.append(
            copies.start(cache.at[sibling, kv], buf.at[pl.ds(8 + 2 * blk, 2)], (seq, sibling))
        )
        for flip in range(2):
            for swap in range(2):
                yh_ = yh + flip - 2 * flip * yh
                other = (1 - yl) * 2 + core + swap - 2 * swap * core
                cache_in.append(
                    copies.start(
                        cache.at[other, kv, yh],
                        buf.at[8 + 2 * blk + yh],
                        at(yh_, z, x, other),
                    )
                )
        buf[pl.ds(8 + 2 * blk, 2)] = cache[blk, kv]

    wait_vz(1)
    send_vz(2)
    wait_kz(1)
    send_kz(2)

    def chain(g, state):
        tile = trecv[g, pl.ds(SLICE, 16)].astype(F32)
        return state * tall(tile[0:8] + tile[8:16], SLICE) + trecv[g, pl.ds(0, SLICE)].astype(F32)

    def earlier(g, state):
        t_arrival(g).wait_recv()
        return chain(g, state)

    each(1, QZ, lambda d: t_arrival(quarter_group(d)).wait_recv())
    state = lax.fori_loop(0, first_group, earlier, jnp.zeros((SLICE, T), F32))
    for i in range(QZ):
        psend[i] = state.astype(BF)
        if i < QZ - 1:
            state = chain(first_group + i, state)

    def p_copy(d):
        z_, device = quarter_peer(d)
        return pltpu.make_async_remote_copy(
            src_ref=psend.at[z_],
            dst_ref=precv.at[x, zq],
            send_sem=pssem.at[d],
            recv_sem=prsem.at[d],
            device_id=device,
            device_id_type=MESH,
        )

    each(1, QZ * NX, lambda d: p_copy(d).start())
    precv[x, zq] = psend[zq]

    wait_vz(2)
    send_vz(3)
    send_vx(1)
    send_vx(7)
    wait_kz(2)
    send_kz(3)

    col = lax.broadcasted_iota(jnp.int32, (8, CHUNK), 1)
    visible_to = 512 * (z + 1)
    bias[0] = jnp.where((col < x * T) | ((col >= 512) & (col < visible_to)), 0.0, NEG)
    bias[1] = jnp.where(col + CHUNK < visible_to, 0.0, NEG)
    for c in range(2):
        bias[2 + c] = jnp.where(
            ((col < 1024) & (col < lens_ref[2 * c]))
            | ((col >= 1024) & (col - 1024 < lens_ref[2 * c + 1])),
            0.0,
            NEG,
        )
    bias[4] = jnp.zeros((8, CHUNK), F32)

    wait_vz(3)
    send_vz(4)
    send_vx(2)
    send_vx(6)

    for copy in sx:
        copy.wait_recv()
    loads[3].wait()
    loads[7].wait()
    each(1, QZ * NX, lambda d: p_copy(d).wait_recv())

    def q_copy(h):
        rows_ = pl.ds(h * T, T)
        return pltpu.make_async_remote_copy(
            src_ref=qown.at[rows_],
            dst_ref=qpar.at[rows_],
            send_sem=xsem.at[h],
            recv_sem=xrsem.at[h],
            device_id=y_partner,
            device_id_type=MESH,
        )

    def back_copies(half):
        rows_ = pl.ds(half * (ROWS // 2), ROWS // 2)
        pairs = [
            (part_out.at[rows_], part_out_in.at[rows_]),
            (part_stat.at[half], part_stat_in.at[half]),
        ]
        return [
            pltpu.make_async_remote_copy(
                src_ref=src,
                dst_ref=dst,
                send_sem=xsem.at[HEADS + 2 * half + i],
                recv_sem=xrsem.at[HEADS + 2 * half + i],
                device_id=y_partner,
                device_id_type=MESH,
            )
            for i, (src, dst) in enumerate(pairs)
        ]

    for h in range(HEADS):
        cols, rows_ = pl.ds(h * T, T), pl.ds(h * T, T)
        pair, k = h // 2, h % 2
        before = precv[pair, pl.ds(QZ // 2 * k, QZ // 2)].reshape(T, T).astype(F32)
        tile = decay_of(srecv[pair, pl.ds(2 * T, 32)])[k]
        state = before * tall(tile, T) + srecv[pair, pl.ds(k * T, T)].astype(F32)
        carried = dot(lq[:, cols], state.astype(BF))
        light = within[h] + expcol[h] * carried
        mean = jnp.mean(light * light, axis=1, keepdims=True)
        out = (light * lax.rsqrt(mean + EPS) * gain[h : h + 1, :]).astype(BF)
        lout[:, cols] = out
        query = rotate(sq[:, cols].astype(F32) + out.astype(F32)).astype(BF)
        qown[rows_, :] = query
        high, low = split2(query.astype(F32) * SCALE)
        qhl[0, rows_, pl.ds(0, T)] = high
        qhl[0, rows_, pl.ds(T, T)] = low

    @pl.when(yh == 1)
    def _():
        each(0, HEADS, lambda h: q_copy(h).start())

    lout_out = pltpu.make_async_copy(lout, lout_ref, lsem.at[9])
    lout_out.start()

    own_k, own_v = ks[0, x], vs[0, x]
    own_k2 = jnp.concatenate([own_k, own_k], axis=1)
    own_v2 = jnp.concatenate([own_v, jnp.ones_like(own_v)], axis=1)
    for h in range(HEADS):
        rows_ = pl.ds(h * T, T)
        scores = jnp.where(causal, nt_dot(qhl[0, rows_, :], own_k2), NEG)
        peak = jnp.broadcast_to(jnp.max(scores, axis=1, keepdims=True), (T, T))
        m_ref[0, rows_, :] = peak
        acc_ref[0, rows_, :] = dot(jnp.exp2(scores - peak).astype(BF), own_v2)

    @pl.when(yh == 0)
    def _():
        m_ref[1] = jnp.full((ROWS, T), NEG, F32)
        acc_ref[1] = jnp.zeros((ROWS, 2 * T), F32)

    wait_kz(3)
    send_kz(4)
    wait_vz(4)
    send_vx(3)
    send_vx(5)
    send_vx(4)
    for copy in cache_in:
        copy.wait_recv()

    def finish_rows(which, h):
        rows_ = pl.ds(h * T, T)
        return m_ref[which, rows_, :], acc_ref[which, rows_, 0:T], acc_ref[which, rows_, T : 2 * T]

    late = z // 4

    def job(v, carry):
        which = (1 - yh) * lax.rem(v // 2, 2)
        chunk = lax.rem(v, 2) + 2 * ((5 - v) // 4)
        mask = chunk + which * (4 - chunk)
        half = v - 2

        @pl.when(v == 2)
        def _():
            wait_kz(4)
            for copy in vx:
                copy.wait_recv()

        for i in range(2):

            @pl.when((yh == 0) & (v == 2 + i))
            def _():
                each(4 * i, 4 * i + 4, lambda h: q_copy(h).wait_recv())
                rows_ = pl.ds(i * (ROWS // 2), ROWS // 2)
                high, low = split2(qpar[rows_].astype(F32) * SCALE)
                qhl[1, rows_, pl.ds(0, T)] = high
                qhl[1, rows_, pl.ds(T, T)] = low

        def place(step):
            own, other = step * RB, half * (ROWS // 2) + step % 2 * RB
            start_row = pl.multiple_of((1 - which) * own + which * other, RB)
            return pl.ds(start_row, RB), (1 - which) * chunk + which * (step // 2)

        def score(step):
            rows_, part = place(step)
            keys = ks[pl.ds(4 * part, 4)].reshape(CHUNK, T)
            return nt_dot(qhl[which, rows_, :], jnp.concatenate([keys, keys], axis=1))

        shade = bias[mask, 0:1, :]
        steps = ROWS // RB
        s_buf[0] = score(0)
        for r in range(steps):
            rows_, part = place(r)
            if r < steps - 1:
                s_buf[(r + 1) % 2] = score(r + 1)
            values = vs[pl.ds(4 * part, 4)].reshape(CHUNK, T)
            values2 = jnp.concatenate([values, jnp.ones_like(values)], axis=1)
            scores = s_buf[r % 2] + shade
            best = scores[:, 0:T]
            for c in range(1, CHUNK // T):
                best = jnp.maximum(best, scores[:, c * T : (c + 1) * T])
            old = m_ref[which, rows_, :]
            new = jnp.maximum(old, jnp.max(best, axis=1, keepdims=True))
            shrink = jnp.exp2(old - new)
            m_ref[which, rows_, :] = new
            weights = jnp.exp2(scores - jnp.concatenate([new] * (CHUNK // T), axis=1)).astype(BF)
            acc_ref[which, rows_, :] = acc_ref[which, rows_, :] * jnp.concatenate(
                [shrink, shrink], axis=1
            ) + dot(weights, values2)

        for i in range(2):

            @pl.when((yh == 0) & (v == 2 + i))
            def _():
                stats = []
                for h in range(4 * i, 4 * i + 4):
                    peak, top, total = finish_rows(1, h)
                    part_out[pl.ds(h * T, T), :] = (top / total).astype(BF)
                    stats.append((peak + jnp.log2(total)).T[0:1, :])
                part_stat[i] = jnp.concatenate(stats + stats, axis=0)
                for copy in back_copies(i):
                    copy.start()

        return carry

    lax.fori_loop(0, 5 + late - 2 * yh, job, 0)

    @pl.when(yh == 0)
    def _():
        for h in range(HEADS):
            _, top, total = finish_rows(0, h)
            att[:, pl.ds(h * T, T)] = (top / total).astype(BF)
        for copy in back_copies(0) + back_copies(1):
            copy.wait_send()

    @pl.when(yh == 1)
    def _():
        each(0, HEADS, lambda h: q_copy(h).wait_send())
        for copy in back_copies(0) + back_copies(1):
            copy.wait_recv()
        for h in range(HEADS):
            peak, top, total = finish_rows(0, h)
            other = jnp.broadcast_to(part_stat_in[h // 4, pl.ds(h % 4, 1), :], (T, T)).T
            best = jnp.maximum(peak, other)
            mine, theirs = jnp.exp2(peak - best), jnp.exp2(other - best)
            merged = top * mine + part_out_in[pl.ds(h * T, T), :].astype(F32) * theirs
            att[:, pl.ds(h * T, T)] = (merged / (total * mine + theirs)).astype(BF)

    att_out = pltpu.make_async_copy(att, att_ref, lsem.at[10])
    att_out.start()
    each(1, QZ, lambda d: t_copy(quarter_group(d)).wait_send())
    each(first_group + QZ, GROUPS, lambda g: t_copy(g).wait_send())
    each(1, QZ * NX, lambda d: p_copy(d).wait_send())
    copies.finish()
    lout_out.wait()
    att_out.wait()


def emit(a_ref, b_ref, a_out, b_out, a_held, b_held, sem):
    pairs = ((a_ref, a_held, a_out), (b_ref, b_held, b_out))
    ins = [pltpu.make_async_copy(src, held, sem.at[i]) for i, (src, held, _) in enumerate(pairs)]
    outs = [
        pltpu.make_async_copy(held, dst, sem.at[2 + i]) for i, (_, held, dst) in enumerate(pairs)
    ]
    for move in ins:
        move.start()
    for i in range(2):
        ins[i].wait()
        outs[i].start()
    for move in outs:
        move.wait()


def per_device(lq, lk, lv, ld, gain, sq, skv, cache, lens, start):
    any_space = pl.BlockSpec(memory_space=pl.ANY)
    smem = pl.BlockSpec(memory_space=pltpu.SMEM)
    rates = np.zeros((8, T), np.float32)
    rates[:, 0:32] = RATES
    rates[:, 32:64] = RATES
    scratch = [
        pltpu.VMEM((T, ROWS), BF),
        pltpu.VMEM((T, ROWS), BF),
        pltpu.VMEM((T, ROWS), BF),
        pltpu.VMEM((T, ROWS), BF),
        pltpu.VMEM((8 * 1024, T), BF),
        pltpu.VMEM((4, 2, 2, NX, T, T), BF),
        pltpu.VMEM((16, NX, T, T), BF),
        pltpu.VMEM((16, NX, T, T), BF),
        pltpu.VMEM((HEADS, T, T), F32),
        pltpu.VMEM((HEADS, T, T), F32),
        pltpu.VMEM((NX, 2 * T + 32, T), BF),
        pltpu.VMEM((NX, 2 * T + 32, T), BF),
        pltpu.VMEM((QZ, SLICE + 16, T), BF),
        pltpu.VMEM((GROUPS, SLICE + 16, T), BF),
        pltpu.VMEM((QZ, SLICE, T), BF),
        pltpu.VMEM((NX, QZ, SLICE, T), BF),
        pltpu.VMEM((NX, 2 * T + 32, T), BF),
        pltpu.VMEM((NX, 2 * T + 32, T), BF),
        pltpu.VMEM((ROWS, T), BF),
        pltpu.VMEM((ROWS, T), BF),
        pltpu.VMEM((2, ROWS, 2 * T), BF),
        pltpu.VMEM((5, 8, CHUNK), F32),
        pltpu.VMEM((2, ROWS, T), F32),
        pltpu.VMEM((2, ROWS, 2 * T), F32),
        pltpu.VMEM((2, RB, CHUNK), F32),
        pltpu.VMEM((ROWS, T), BF),
        pltpu.VMEM((2, 8, T), F32),
        pltpu.VMEM((ROWS, T), BF),
        pltpu.VMEM((2, 8, T), F32),
        pltpu.VMEM((T, ROWS), BF),
        pltpu.VMEM((T, ROWS), BF),
        pltpu.VMEM((HEADS, T), F32),
        pltpu.VMEM((2 * T, T), BF),
        pltpu.VMEM((HEADS, T), F32),
        pltpu.VMEM((8, T), F32),
        pltpu.SemaphoreType.DMA((11,)),
        pltpu.SemaphoreType.DMA((N_COPIES,)),
        pltpu.SemaphoreType.DMA((N_COPIES,)),
        pltpu.SemaphoreType.DMA((GROUPS,)),
        pltpu.SemaphoreType.DMA((GROUPS,)),
        pltpu.SemaphoreType.DMA((QZ * NX,)),
        pltpu.SemaphoreType.DMA((QZ * NX,)),
        pltpu.SemaphoreType.DMA((4 + HEADS,)),
        pltpu.SemaphoreType.DMA((4 + HEADS,)),
        pltpu.SemaphoreType.REGULAR,
    ]
    results = pl.pallas_call(
        kernel,
        out_shape=(
            jax.ShapeDtypeStruct((T, ROWS), BF),
            jax.ShapeDtypeStruct((T, ROWS), BF),
        ),
        in_specs=[any_space] * 9 + [smem, smem],
        out_specs=(any_space, any_space),
        scratch_shapes=scratch,
        compiler_params=pltpu.CompilerParams(
            collective_id=0, has_side_effects=True, vmem_limit_bytes=60 * 2**20
        ),
    )(
        lq,
        lk,
        lv,
        ld,
        gain.reshape(HEADS, T),
        sq,
        skv.reshape(2 * T, T),
        cache.reshape(8 * 1024, T),
        jnp.asarray(rates),
        lens,
        start,
    )
    return pl.pallas_call(
        emit,
        out_shape=tuple(jax.ShapeDtypeStruct(r.shape, r.dtype) for r in results),
        in_specs=[any_space, any_space],
        out_specs=(any_space, any_space),
        scratch_shapes=[pltpu.VMEM((T, ROWS), BF), pltpu.VMEM((T, ROWS), BF), pltpu.SemaphoreType.DMA((4,))],
    )(*results)


def solution(mesh):
    in_specs = (
        P("seq", "blk"),
        P("seq", "blk"),
        P("seq", "blk"),
        P("blk", "seq"),
        P("blk"),
        P("seq", "blk"),
        P("seq", None, "blk", None),
        P("blk", None, None, None),
        P(),
        P(),
    )
    out_specs = (P("seq", "blk"), P("seq", "blk"))
    return jax.shard_map(
        per_device, mesh=mesh, in_specs=in_specs, out_specs=out_specs, check_vma=False
    )
```

```python
import math

import jax
import jax.numpy as jnp
import numpy as np
from jax import lax
from jax.experimental import pallas as pl
from jax.experimental.pallas import tpu as pltpu
from jax.sharding import PartitionSpec as P

MESH = pl.DeviceIdType.MESH
BF = jnp.bfloat16
F32 = jnp.float32
EPS = 1e-06
SCALE = np.float32(1.4426950408889634 / math.sqrt(128.0))
RATES = (10000000.0 ** (-np.arange(32) / 32.0)).astype(np.float32)
NEG = -1e30

T = 128
HEADS = 8
ROWS = HEADS * T
CHUNK = 2048
RB = 256
NX, NZ = 4, 8
QZ = 4
SLICE = 2 * T // QZ
GROUPS = 16


def nt_dot(a, b):
    return lax.dot_general(a, b, (((1,), (1,)), ((), ())), preferred_element_type=F32)


def dot(a, b):
    return jnp.dot(a, b, preferred_element_type=F32)


def split2(value):
    high = value.astype(BF)
    return high, (value - high.astype(F32)).astype(BF)


class Copies:
    def __init__(self, send_sem, recv_sem):
        self.send_sem, self.recv_sem = send_sem, recv_sem
        self.made = []

    def make(self, src, dst, to):
        number = len(self.made)
        copy = pltpu.make_async_remote_copy(
            src_ref=src,
            dst_ref=dst,
            send_sem=self.send_sem.at[number],
            recv_sem=self.recv_sem.at[number],
            device_id=to,
            device_id_type=MESH,
        )
        self.made.append(copy)
        return copy

    def start(self, src, dst, to):
        copy = self.make(src, dst, to)
        copy.start()
        return copy

    def finish(self):
        for copy in self.made:
            copy.wait_send()


N_COPIES = 64


def one_hot(major, minor):
    size = major * minor
    out = lax.broadcasted_iota(jnp.int32, (size, size), 0)
    source = lax.broadcasted_iota(jnp.int32, (size, size), 1)
    wanted = lax.rem(out, minor) * major + out // minor
    return jnp.where(source == wanted, 1.0, 0.0).astype(BF)


def kernel(
    lq_hbm,
    lk_hbm,
    lv_hbm,
    ld_hbm,
    gain_hbm,
    sq_hbm,
    skv_hbm,
    cache_hbm,
    rates_hbm,
    lens_ref,
    start_ref,
    lout_ref,
    att_ref,
    lq,
    lk,
    lv,
    sq,
    cache_raw,
    cache,
    kv,
    within,
    expcol,
    lsend,
    lrecv,
    tsend,
    trecv,
    psend,
    precv,
    ssend,
    srecv,
    qown,
    qpar,
    qhl,
    bias,
    m_ref,
    acc_ref,
    s_buf,
    part_out,
    part_stat,
    part_out_in,
    part_stat_in,
    lout,
    att,
    ld,
    skv,
    gain,
    rates,
    lsem,
    ssem,
    rsem,
    tssem,
    trsem,
    pssem,
    prsem,
    xsem,
    xrsem,
    ready,
):
    seq, blk = lax.axis_index("seq"), lax.axis_index("blk")
    x = lax.rem(seq, NX)
    z = lax.rem(seq // NX, NZ)
    yh = seq // (NX * NZ)
    yl, core = blk // 2, lax.rem(blk, 2)

    def at(yh_, z_, x_, blk_):
        return ((yh_ * NZ + z_) * NX + x_, blk_)

    def x_peer(d):
        return at(yh, z, lax.rem(x + d, NX), blk)

    group = yh * NZ + z
    quarter, zq = group // QZ, lax.rem(z, QZ)
    first_group = quarter * QZ

    def quarter_peer(d):
        place = lax.rem(zq * NX + x + d, QZ * NX)
        return place // NX, at(0, first_group + place // NX, lax.rem(place, NX), blk)

    def column(g):
        return at(0, g, x, blk)

    up, down = at(yh, lax.rem(z + 1, NZ), x, blk), at(yh, lax.rem(z + NZ - 1, NZ), x, blk)
    sibling = blk + 1 - 2 * core
    y_partner = at(1 - yh, z, x, blk)

    def each(first, last, action):
        def one(d, carry):
            action(d)
            return carry

        lax.fori_loop(first, last, one, 0)

    loads = [
        pltpu.make_async_copy(src, dst, lsem.at[i])
        for i, (src, dst) in enumerate(
            [
                (lk_hbm, lk),
                (lv_hbm, lv),
                (lq_hbm, lq),
                (sq_hbm, sq),
                (cache_hbm, cache_raw),
                (ld_hbm, ld),
                (skv_hbm, skv),
                (gain_hbm, gain),
                (rates_hbm, rates),
            ]
        )
    ]
    for i in (5, 0, 1, 6, 8, 2, 4, 3, 7):
        loads[i].start()

    barrier = pltpu.get_barrier_semaphore()

    def greet(device):
        pl.semaphore_signal(barrier, inc=1, device_id=device, device_id_type=MESH)

    each(1, QZ * NX, lambda d: greet(quarter_peer(d)[1]))
    greet((seq, sibling))
    for yh_ in range(2):
        for core_ in range(2):
            greet(at(yh_, z, x, (1 - yl) * 2 + core_))
    each(first_group + QZ, GROUPS, lambda g: greet(column(g)))

    loads[5].wait()
    cumulative = ld[...]
    lane8 = lax.broadcasted_iota(jnp.int32, (HEADS, T), 1)
    shift = 1
    while shift < T:
        cumulative = cumulative + jnp.where(lane8 >= shift, pltpu.roll(cumulative, shift, 1), 0.0)
        shift *= 2
    last = cumulative[:, T - 1 : T]
    tail = jnp.exp(last - cumulative)
    decay_high, decay_low = split2(jnp.broadcast_to(jnp.exp(last), (HEADS, T)))
    loads[0].wait()
    loads[1].wait()
    for h in range(HEADS):
        cols = pl.ds(h * T, T)
        keys_t = lk[:, cols].astype(F32).T * tail[h : h + 1, :]
        local = dot(keys_t.astype(BF), lv[:, cols])
        lsend[h // 2, pl.ds((h % 2) * T, T)] = local.astype(BF)
    for pair in range(NX):
        rows_ = [
            jnp.broadcast_to(part[h : h + 1, :].astype(F32), (8, T))
            for h in (2 * pair, 2 * pair + 1)
            for part in (decay_high, decay_low)
        ]
        lsend[pair, pl.ds(2 * T, 32)] = jnp.concatenate(rows_, axis=0).astype(BF)
    lrecv[x] = lsend[x]

    pl.semaphore_wait(barrier, QZ * NX - 1 + 5 + first_group)
    each(
        0,
        first_group,
        lambda g: pl.semaphore_signal(ready, inc=1, device_id=column(g), device_id_type=MESH),
    )

    copies = Copies(ssem, rsem)
    lx = [
        copies.start(lsend.at[lax.rem(x + d, NX)], lrecv.at[x], x_peer(d)) for d in range(1, NX)
    ]

    lane = lax.broadcasted_iota(jnp.int32, (T, T), 1)
    row = lax.broadcasted_iota(jnp.int32, (T, T), 0)
    loads[8].wait()
    loads[6].wait()
    positions = (start_ref[0] + seq * T + row).astype(F32)
    angles = positions * rates[0:1, :]
    sine = jnp.sin(angles)
    cos_t = jnp.where(lane < 64, jnp.cos(angles), 1.0)
    sin_t = jnp.where(lane < 32, -sine, jnp.where(lane < 64, sine, 0.0))

    def rotate(features):
        partner = jnp.where(lane < 32, pltpu.roll(features, 96, 1), pltpu.roll(features, 32, 1))
        return features * cos_t + partner * sin_t

    span = dot(one_hot(2, T), skv[...])
    kv[0, x, 0] = rotate(span[0:T]).astype(BF)
    kv[0, x, 1] = span[T : 2 * T].astype(BF)

    along_z, along_x = {}, []

    def send_z(step):
        if step < 4:
            moves = [
                copies.start(kv.at[step - 1, x], kv.at[step, x], up),
                copies.start(kv.at[(9 - step) % 8, x], kv.at[8 - step, x], down),
            ]
        else:
            moves = [
                copies.start(kv.at[3, x, 0], kv.at[4, x, 0], up),
                copies.start(kv.at[5, x, 1], kv.at[4, x, 1], down),
            ]
        along_z[step] = moves

    def wait_z(step):
        for copy in along_z[step]:
            copy.wait_recv()

    def send_x(slot):
        for d in range(1, NX):
            along_x.append(copies.start(kv.at[slot, x], kv.at[slot, x], x_peer(d)))

    causal = row >= lane
    loads[2].wait()
    for h in range(HEADS):
        cols = pl.ds(h * T, T)
        across = jnp.broadcast_to(cumulative[h : h + 1, :], (T, T))
        downward = across.T
        weights = jnp.where(causal, jnp.exp(jnp.minimum(downward - across, 0.0)), 0.0)
        scores = nt_dot(lq[:, cols], lk[:, cols])
        within[h] = dot((scores * weights).astype(BF), lv[:, cols])
        expcol[h] = jnp.exp(downward)

    loads[4].wait()
    sort = one_hot(8, 32)

    def relayout(b, carry):
        part = dot(sort, cache_raw[pl.ds(pl.multiple_of(b * 256, 256), 256), :]).astype(BF)
        rows_ = pl.ds(pl.multiple_of(lax.rem(b, 4) * 32, 32), 32)
        for i in range(2):
            for h in range(4):
                at_ = (i * 4 + h) * 32
                cache[h, b // 16, lax.rem(b // 4, 4), i, rows_] = part[at_ : at_ + 32]
        return carry

    lax.fori_loop(0, 32, relayout, 0, unroll=4)

    @pl.when(quarter < 3)
    def _():
        pl.semaphore_wait(ready, GROUPS - QZ - first_group)

    send_z(1)
    send_x(0)

    for copy in lx:
        copy.wait_recv()

    def decay_of(tile):
        wide = tile.astype(F32)
        return [wide[0:8] + wide[8:16], wide[16:24] + wide[24:32]]

    def tall(decay, rows_):
        return jnp.concatenate([decay] * (rows_ // 8), axis=0)

    def two_parts(decay):
        high, low = split2(decay)
        return [high.astype(F32), low.astype(F32)]

    decays = [decay_of(lrecv[i, pl.ds(2 * T, 32)]) for i in range(NX)]
    ones8 = jnp.ones((8, T), F32)
    overall = [ones8, ones8]
    totals = [jnp.zeros((T, T), F32)] * 2
    for i in range(NX):
        for k in range(2):
            ssend[i, pl.ds(k * T, T)] = totals[k].astype(BF)
            totals[k] = totals[k] * tall(decays[i][k], T) + lrecv[i, pl.ds(k * T, T)].astype(F32)
        ssend[i, pl.ds(2 * T, 32)] = jnp.concatenate(
            two_parts(overall[0]) + two_parts(overall[1]), axis=0
        ).astype(BF)
        overall = [overall[k] * decays[i][k] for k in range(2)]
    for k in range(2):
        tail_rows = jnp.concatenate(two_parts(overall[k]), axis=0).astype(BF)
        for i in range(QZ // 2):
            piece = totals[k][SLICE * i : SLICE * (i + 1)]
            tsend[QZ // 2 * k + i, pl.ds(0, SLICE)] = piece.astype(BF)
            tsend[QZ // 2 * k + i, pl.ds(SLICE, 16)] = tail_rows

    def t_copy(g):
        return pltpu.make_async_remote_copy(
            src_ref=tsend.at[lax.rem(g, QZ)],
            dst_ref=trecv.at[group],
            send_sem=tssem.at[g],
            recv_sem=trsem.at[group],
            device_id=column(g),
            device_id_type=MESH,
        )

    def t_arrival(g):
        return pltpu.make_async_remote_copy(
            src_ref=tsend.at[0],
            dst_ref=trecv.at[g],
            send_sem=tssem.at[g],
            recv_sem=trsem.at[g],
            device_id=column(g),
            device_id_type=MESH,
        )

    def quarter_group(d):
        return first_group + lax.rem(zq + d, QZ)

    each(1, QZ, lambda d: t_copy(quarter_group(d)).start())
    each(first_group + QZ, GROUPS, lambda g: t_copy(g).start())
    trecv[group] = tsend[zq]
    sx = [
        copies.start(ssend.at[lax.rem(x + d, NX)], srecv.at[x], x_peer(d)) for d in range(1, NX)
    ]
    srecv[x] = ssend[x]

    cache_in = [
        copies.start(cache.at[sibling], kv.at[pl.ds(8 + 2 * blk, 2)], (seq, sibling))
    ]
    for flip in range(2):
        for swap in range(2):
            yh_ = yh + flip - 2 * flip * yh
            other = (1 - yl) * 2 + core + swap - 2 * swap * core
            cache_in.append(
                copies.start(
                    cache.at[other, yh], kv.at[8 + 2 * blk + yh], at(yh_, z, x, other)
                )
            )
    kv[pl.ds(8 + 2 * blk, 2)] = cache[blk]

    wait_z(1)
    send_z(2)
    send_x(1)
    send_x(7)

    def chain(g, state):
        tile = trecv[g, pl.ds(SLICE, 16)].astype(F32)
        return state * tall(tile[0:8] + tile[8:16], SLICE) + trecv[g, pl.ds(0, SLICE)].astype(F32)

    def earlier(g, state):
        t_arrival(g).wait_recv()
        return chain(g, state)

    each(1, QZ, lambda d: t_arrival(quarter_group(d)).wait_recv())
    state = lax.fori_loop(0, first_group, earlier, jnp.zeros((SLICE, T), F32))
    for i in range(QZ):
        psend[i] = state.astype(BF)
        if i < QZ - 1:
            state = chain(first_group + i, state)

    def p_copy(d):
        z_, device = quarter_peer(d)
        return pltpu.make_async_remote_copy(
            src_ref=psend.at[z_],
            dst_ref=precv.at[x, zq],
            send_sem=pssem.at[d],
            recv_sem=prsem.at[d],
            device_id=device,
            device_id_type=MESH,
        )

    each(1, QZ * NX, lambda d: p_copy(d).start())
    precv[x, zq] = psend[zq]

    wait_z(2)
    send_z(3)
    send_x(2)
    send_x(6)

    col = lax.broadcasted_iota(jnp.int32, (8, CHUNK), 1)
    visible_to = 512 * (z + 1)
    bias[0] = jnp.where((col < x * T) | ((col >= 512) & (col < visible_to)), 0.0, NEG)
    bias[1] = jnp.where(col + CHUNK < visible_to, 0.0, NEG)
    for c in range(2):
        bias[2 + c] = jnp.where(
            ((col < 1024) & (col < lens_ref[2 * c]))
            | ((col >= 1024) & (col - 1024 < lens_ref[2 * c + 1])),
            0.0,
            NEG,
        )
    bias[4] = jnp.zeros((8, CHUNK), F32)

    wait_z(3)
    send_z(4)
    send_x(3)
    send_x(5)

    for copy in sx:
        copy.wait_recv()
    loads[3].wait()
    loads[7].wait()
    each(1, QZ * NX, lambda d: p_copy(d).wait_recv())
    wait_z(4)
    send_x(4)

    def q_copy(h):
        rows_ = pl.ds(h * T, T)
        return pltpu.make_async_remote_copy(
            src_ref=qown.at[rows_],
            dst_ref=qpar.at[rows_],
            send_sem=xsem.at[h],
            recv_sem=xrsem.at[h],
            device_id=y_partner,
            device_id_type=MESH,
        )

    def back_copies(half):
        rows_ = pl.ds(half * (ROWS // 2), ROWS // 2)
        pairs = [
            (part_out.at[rows_], part_out_in.at[rows_]),
            (part_stat.at[half], part_stat_in.at[half]),
        ]
        return [
            pltpu.make_async_remote_copy(
                src_ref=src,
                dst_ref=dst,
                send_sem=xsem.at[HEADS + 2 * half + i],
                recv_sem=xrsem.at[HEADS + 2 * half + i],
                device_id=y_partner,
                device_id_type=MESH,
            )
            for i, (src, dst) in enumerate(pairs)
        ]

    for h in range(HEADS):
        cols, rows_ = pl.ds(h * T, T), pl.ds(h * T, T)
        pair, k = h // 2, h % 2
        before = precv[pair, pl.ds(QZ // 2 * k, QZ // 2)].reshape(T, T).astype(F32)
        tile = decay_of(srecv[pair, pl.ds(2 * T, 32)])[k]
        state = before * tall(tile, T) + srecv[pair, pl.ds(k * T, T)].astype(F32)
        carried = dot(lq[:, cols], state.astype(BF))
        light = within[h] + expcol[h] * carried
        mean = jnp.mean(light * light, axis=1, keepdims=True)
        out = (light * lax.rsqrt(mean + EPS) * gain[h : h + 1, :]).astype(BF)
        lout[:, cols] = out
        query = rotate(sq[:, cols].astype(F32) + out.astype(F32)).astype(BF)
        qown[rows_, :] = query
        high, low = split2(query.astype(F32) * SCALE)
        qhl[0, rows_, pl.ds(0, T)] = high
        qhl[0, rows_, pl.ds(T, T)] = low

    @pl.when(yh == 1)
    def _():
        each(0, HEADS, lambda h: q_copy(h).start())

    lout_out = pltpu.make_async_copy(lout, lout_ref, lsem.at[9])
    lout_out.start()

    own_k, own_v = kv[0, x, 0], kv[0, x, 1]
    own_k2 = jnp.concatenate([own_k, own_k], axis=1)
    own_v2 = jnp.concatenate([own_v, jnp.ones_like(own_v)], axis=1)
    for h in range(HEADS):
        rows_ = pl.ds(h * T, T)
        scores = jnp.where(causal, nt_dot(qhl[0, rows_, :], own_k2), NEG)
        peak = jnp.broadcast_to(jnp.max(scores, axis=1, keepdims=True), (T, T))
        m_ref[0, rows_, :] = peak
        acc_ref[0, rows_, :] = dot(jnp.exp2(scores - peak).astype(BF), own_v2)

    @pl.when(yh == 0)
    def _():
        m_ref[1] = jnp.full((ROWS, T), NEG, F32)
        acc_ref[1] = jnp.zeros((ROWS, 2 * T), F32)

    for copy in cache_in:
        copy.wait_recv()

    def finish_rows(which, h):
        rows_ = pl.ds(h * T, T)
        return m_ref[which, rows_, :], acc_ref[which, rows_, 0:T], acc_ref[which, rows_, T : 2 * T]

    late = z // 4

    def job(v, carry):
        which = (1 - yh) * lax.rem(v // 2, 2)
        chunk = lax.rem(v, 2) + 2 * ((5 - v) // 4)
        mask = chunk + which * (4 - chunk)
        half = v - 2

        @pl.when(v == 2)
        def _():
            for copy in along_x:
                copy.wait_recv()

        for i in range(2):

            @pl.when((yh == 0) & (v == 2 + i))
            def _():
                each(4 * i, 4 * i + 4, lambda h: q_copy(h).wait_recv())
                rows_ = pl.ds(i * (ROWS // 2), ROWS // 2)
                high, low = split2(qpar[rows_].astype(F32) * SCALE)
                qhl[1, rows_, pl.ds(0, T)] = high
                qhl[1, rows_, pl.ds(T, T)] = low

        def place(step):
            own, other = step * RB, half * (ROWS // 2) + step % 2 * RB
            start_row = pl.multiple_of((1 - which) * own + which * other, RB)
            return pl.ds(start_row, RB), (1 - which) * chunk + which * (step // 2)

        def score(step):
            rows_, part = place(step)
            keys = kv[pl.ds(4 * part, 4), :, 0].reshape(CHUNK, T)
            return nt_dot(qhl[which, rows_, :], jnp.concatenate([keys, keys], axis=1))

        shade = bias[mask, 0:1, :]
        steps = ROWS // RB
        s_buf[0] = score(0)
        for r in range(steps):
            rows_, part = place(r)
            if r < steps - 1:
                s_buf[(r + 1) % 2] = score(r + 1)
            values = kv[pl.ds(4 * part, 4), :, 1].reshape(CHUNK, T)
            values2 = jnp.concatenate([values, jnp.ones_like(values)], axis=1)
            scores = s_buf[r % 2] + shade
            best = scores[:, 0:T]
            for c in range(1, CHUNK // T):
                best = jnp.maximum(best, scores[:, c * T : (c + 1) * T])
            old = m_ref[which, rows_, :]
            new = jnp.maximum(old, jnp.max(best, axis=1, keepdims=True))
            shrink = jnp.exp2(old - new)
            m_ref[which, rows_, :] = new
            weights = jnp.exp2(scores - jnp.concatenate([new] * (CHUNK // T), axis=1)).astype(BF)
            acc_ref[which, rows_, :] = acc_ref[which, rows_, :] * jnp.concatenate(
                [shrink, shrink], axis=1
            ) + dot(weights, values2)

        for i in range(2):

            @pl.when((yh == 0) & (v == 2 + i))
            def _():
                stats = []
                for h in range(4 * i, 4 * i + 4):
                    peak, top, total = finish_rows(1, h)
                    part_out[pl.ds(h * T, T), :] = (top / total).astype(BF)
                    stats.append((peak + jnp.log2(total)).T[0:1, :])
                part_stat[i] = jnp.concatenate(stats + stats, axis=0)
                for copy in back_copies(i):
                    copy.start()

        return carry

    lax.fori_loop(0, 5 + late - 2 * yh, job, 0)

    @pl.when(yh == 0)
    def _():
        for h in range(HEADS):
            _, top, total = finish_rows(0, h)
            att[:, pl.ds(h * T, T)] = (top / total).astype(BF)
        for copy in back_copies(0) + back_copies(1):
            copy.wait_send()

    @pl.when(yh == 1)
    def _():
        each(0, HEADS, lambda h: q_copy(h).wait_send())
        for copy in back_copies(0) + back_copies(1):
            copy.wait_recv()
        for h in range(HEADS):
            peak, top, total = finish_rows(0, h)
            other = jnp.broadcast_to(part_stat_in[h // 4, pl.ds(h % 4, 1), :], (T, T)).T
            best = jnp.maximum(peak, other)
            mine, theirs = jnp.exp2(peak - best), jnp.exp2(other - best)
            merged = top * mine + part_out_in[pl.ds(h * T, T), :].astype(F32) * theirs
            att[:, pl.ds(h * T, T)] = (merged / (total * mine + theirs)).astype(BF)

    att_out = pltpu.make_async_copy(att, att_ref, lsem.at[10])
    att_out.start()
    each(1, QZ, lambda d: t_copy(quarter_group(d)).wait_send())
    each(first_group + QZ, GROUPS, lambda g: t_copy(g).wait_send())
    each(1, QZ * NX, lambda d: p_copy(d).wait_send())
    copies.finish()
    lout_out.wait()
    att_out.wait()


def emit(a_ref, b_ref, a_out, b_out, a_held, b_held, sem):
    ins, outs = [], []
    size = T // 4
    for part in range(4):
        rows_ = pl.ds(part * size, size)
        for src, held, dst in ((a_ref, a_held, a_out), (b_ref, b_held, b_out)):
            number = len(ins)
            ins.append(pltpu.make_async_copy(src.at[rows_], held.at[rows_], sem.at[0, number]))
            outs.append(pltpu.make_async_copy(held.at[rows_], dst.at[rows_], sem.at[1, number]))
    for move in ins:
        move.start()
    for i, move in enumerate(ins):
        move.wait()
        outs[i].start()
    for move in outs:
        move.wait()


def per_device(lq, lk, lv, ld, gain, sq, skv, cache, lens, start):
    any_space = pl.BlockSpec(memory_space=pl.ANY)
    smem = pl.BlockSpec(memory_space=pltpu.SMEM)
    rates = np.zeros((8, T), np.float32)
    rates[:, 0:32] = RATES
    rates[:, 32:64] = RATES
    scratch = [
        pltpu.VMEM((T, ROWS), BF),
        pltpu.VMEM((T, ROWS), BF),
        pltpu.VMEM((T, ROWS), BF),
        pltpu.VMEM((T, ROWS), BF),
        pltpu.VMEM((8 * 1024, T), BF),
        pltpu.VMEM((4, 2, NX, 2, T, T), BF),
        pltpu.VMEM((16, NX, 2, T, T), BF),
        pltpu.VMEM((HEADS, T, T), F32),
        pltpu.VMEM((HEADS, T, T), F32),
        pltpu.VMEM((NX, 2 * T + 32, T), BF),
        pltpu.VMEM((NX, 2 * T + 32, T), BF),
        pltpu.VMEM((QZ, SLICE + 16, T), BF),
        pltpu.VMEM((GROUPS, SLICE + 16, T), BF),
        pltpu.VMEM((QZ, SLICE, T), BF),
        pltpu.VMEM((NX, QZ, SLICE, T), BF),
        pltpu.VMEM((NX, 2 * T + 32, T), BF),
        pltpu.VMEM((NX, 2 * T + 32, T), BF),
        pltpu.VMEM((ROWS, T), BF),
        pltpu.VMEM((ROWS, T), BF),
        pltpu.VMEM((2, ROWS, 2 * T), BF),
        pltpu.VMEM((5, 8, CHUNK), F32),
        pltpu.VMEM((2, ROWS, T), F32),
        pltpu.VMEM((2, ROWS, 2 * T), F32),
        pltpu.VMEM((2, RB, CHUNK), F32),
        pltpu.VMEM((ROWS, T), BF),
        pltpu.VMEM((2, 8, T), F32),
        pltpu.VMEM((ROWS, T), BF),
        pltpu.VMEM((2, 8, T), F32),
        pltpu.VMEM((T, ROWS), BF),
        pltpu.VMEM((T, ROWS), BF),
        pltpu.VMEM((HEADS, T), F32),
        pltpu.VMEM((2 * T, T), BF),
        pltpu.VMEM((HEADS, T), F32),
        pltpu.VMEM((8, T), F32),
        pltpu.SemaphoreType.DMA((11,)),
        pltpu.SemaphoreType.DMA((N_COPIES,)),
        pltpu.SemaphoreType.DMA((N_COPIES,)),
        pltpu.SemaphoreType.DMA((GROUPS,)),
        pltpu.SemaphoreType.DMA((GROUPS,)),
        pltpu.SemaphoreType.DMA((QZ * NX,)),
        pltpu.SemaphoreType.DMA((QZ * NX,)),
        pltpu.SemaphoreType.DMA((4 + HEADS,)),
        pltpu.SemaphoreType.DMA((4 + HEADS,)),
        pltpu.SemaphoreType.REGULAR,
    ]
    results = pl.pallas_call(
        kernel,
        out_shape=(
            jax.ShapeDtypeStruct((T, ROWS), BF),
            jax.ShapeDtypeStruct((T, ROWS), BF),
        ),
        in_specs=[any_space] * 9 + [smem, smem],
        out_specs=(any_space, any_space),
        scratch_shapes=scratch,
        compiler_params=pltpu.CompilerParams(
            collective_id=0, has_side_effects=True, vmem_limit_bytes=60 * 2**20
        ),
    )(
        lq,
        lk,
        lv,
        ld,
        gain.reshape(HEADS, T),
        sq,
        skv.reshape(2 * T, T),
        cache.reshape(8 * 1024, T),
        jnp.asarray(rates),
        lens,
        start,
    )
    return pl.pallas_call(
        emit,
        out_shape=tuple(jax.ShapeDtypeStruct(r.shape, r.dtype) for r in results),
        in_specs=[any_space, any_space],
        out_specs=(any_space, any_space),
        scratch_shapes=[pltpu.VMEM((T, ROWS), BF), pltpu.VMEM((T, ROWS), BF), pltpu.SemaphoreType.DMA((2, 8))],
    )(*results)


def solution(mesh):
    in_specs = (
        P("seq", "blk"),
        P("seq", "blk"),
        P("seq", "blk"),
        P("blk", "seq"),
        P("blk"),
        P("seq", "blk"),
        P("seq", None, "blk", None),
        P("blk", None, None, None),
        P(),
        P(),
    )
    out_specs = (P("seq", "blk"), P("seq", "blk"))
    return jax.shard_map(
        per_device, mesh=mesh, in_specs=in_specs, out_specs=out_specs, check_vma=False
    )
```
